32 devices in a mesh: elem: 8 (over z, y), snap: 4 (over x, core).
Axes of the slice: x: 2, y: 2, z: 4, core: 2. Of those that a mesh axis runs over, the one named last changes fastest.
Arguments:
- node_basis: bfloat16 [8192, 1536], P('elem'), may hold values from -0.25 to 0.25
- stiff_terms: bfloat16 [16, 24, 24], replicated, may hold values from -1.25 to 1.25
- reduced_coords: bfloat16 [512, 32], P(None, 'snap'), may hold values from -6 to 6
- sample_list: int32 [64], replicated, may hold values from 0 to 255, as said below
- connectivity: int32 [256, 8], replicated, may hold values from -1 to 8191, as said below
- node_slot: int32 [8192], replicated, may hold values from 0 to 8191, as said below
- elem_device: int32 [64], replicated, may hold values from 0 to 7, as said below
Outputs:
- ortho_panel: float32 [128, 512, 512], P('elem', 'snap')
- triangle_factor: float32 [512, 512], P('elem')
The draws below stay inside these ranges and needn't reach their ends.
Inputs may be any that keep to these rules, and one draw needn't show every extreme that they name: `sample_list`: distinct element ids. `connectivity`: each element lists 4, 6 or 8 live nodes first and -1 after them; the live nodes of one element are owned by distinct indices of elem (owner = node_slot // 1024); for every index d of elem and every owner o, at most 16 sampled elements computed on d have a live node owned by o, and some pair (d, o) reaches 16. `node_slot`: a permutation. `elem_device`: each index of elem computes at most 16 sampled elements; some index computes exactly 16.
All inputs are finite; a program needn't handle non-finite values.
Results may differ from the reference program's by a relative error of at most 0.0056.
Values may be sent and summed in bfloat16 or wider, within the bound.
No kernel may reach another device: no remote copies, remote signals or barrier semaphores. Data moves between devices by JAX's collectives and lax.ppermute only.
A program may use at most 64 MiB of HBM per device.

```python
import jax
import jax.numpy as jnp
from jax import lax

MODES = 512
TERMS = 16
SNAPS = 32
ENODES = 8
NDOF = 3
EL_DEV = 8
NODE_DEV = 1024
CAP = 16
SAMPLED = 64
ELEMS = 256
NODES = 8192
COLS = 512
N_ELEM = 8


def build_tables(key):
    subkeys = [jax.random.fold_in(key, 101 + number) for number in range(10)]
    sampled_ids = jax.random.permutation(subkeys[0], ELEMS)[:SAMPLED].astype(jnp.int32)
    halves = N_ELEM // 2
    extra_count = jax.random.randint(subkeys[1], (halves,), 0, CAP + 1).astype(jnp.int32).at[0].set(0)
    paired = jnp.stack([CAP - extra_count, extra_count], axis=1).reshape(N_ELEM)
    device_order = jax.random.permutation(subkeys[2], N_ELEM).astype(jnp.int32)
    counts = jnp.zeros((N_ELEM,), jnp.int32).at[device_order].set(paired)
    bounds = jnp.cumsum(counts)
    position_rank = jax.random.permutation(subkeys[3], SAMPLED).astype(jnp.int32)
    assigned = jnp.sum((bounds[None, :] <= position_rank[:, None]).astype(jnp.int32), axis=1).astype(jnp.int32)
    position_ids = jnp.arange(SAMPLED, dtype=jnp.int32)
    earlier = (position_ids[None, :] < position_ids[:, None]) & (assigned[None, :] == assigned[:, None])
    slots = jnp.sum(earlier.astype(jnp.int32), axis=1).astype(jnp.int32)
    slot_table = jax.random.permutation(subkeys[4], NODES).astype(jnp.int32)
    inverse = jnp.zeros((NODES,), jnp.int32).at[slot_table].set(jnp.arange(NODES, dtype=jnp.int32))
    owner_ids = jnp.arange(N_ELEM, dtype=jnp.int32)
    cycle_scores = jax.random.randint(subkeys[5], (N_ELEM, N_ELEM), 0, 1 << 20) * N_ELEM + owner_ids[None, :]
    cycles = jnp.argsort(cycle_scores, axis=1).astype(jnp.int32)
    positions = jnp.arange(ENODES, dtype=jnp.int32)
    cycle_index = (slots[:, None] * ENODES + positions[None, :]) % N_ELEM
    sampled_owners = cycles[assigned[:, None], cycle_index]
    scores = jax.random.randint(subkeys[6], (ELEMS, N_ELEM), 0, 1 << 20) * N_ELEM + owner_ids[None, :]
    owner_pick = jnp.argsort(scores, axis=1)[:, :ENODES].astype(jnp.int32)
    owner_pick = owner_pick.at[sampled_ids].set(sampled_owners)
    local_pick = jax.random.randint(subkeys[7], (ELEMS, ENODES), 0, NODE_DEV).astype(jnp.int32)
    node_ids = inverse[owner_pick * NODE_DEV + local_pick]
    elem_kinds = jax.random.randint(subkeys[8], (ELEMS,), 0, 3).astype(jnp.int32)
    linked = jnp.where(positions[None, :] < (4 + 2 * elem_kinds)[:, None], node_ids, -1).astype(jnp.int32)
    return (sampled_ids, linked, slot_table, assigned)


def draw_sample_list(key, part):
    return build_tables(key)[0]


def draw_connectivity(key, part):
    return build_tables(key)[1]


def draw_node_slot(key, part):
    return build_tables(key)[2]


def draw_elem_device(key, part):
    return build_tables(key)[3]


def shard_levels(own_key, shape, shards, low, largest):
    level, own = 1.0, jax.random.fold_in(own_key, 6)
    for axis_at, shards_of in shards:
        heights = jnp.exp(jax.random.uniform(jax.random.fold_in(own, axis_at), (shards_of,), jnp.float32, low / len(shards), largest / len(shards)))
        level = level * jnp.repeat(heights, shape[axis_at] // shards_of).reshape([-1 if axis == axis_at else 1 for axis in range(len(shape))])
    return level


def scatter_about(stream_key, extent, width, most, cuts=(), kind=jnp.bfloat16):
    factor_of = shard_levels(stream_key, extent, cuts, -0.22, 0.18) if cuts else 1.0
    entries = jax.random.normal(stream_key, extent, jnp.float32) * width * factor_of
    return jnp.minimum(jnp.maximum(entries, -most), most).astype(kind)


def setup_inputs(seed: int = 0) -> dict:
    key_of = jax.random.split(jax.random.key(seed), 8)
    node_basis = scatter_about(key_of[0], (NODES, NDOF * MODES), MODES ** -0.5, 0.25, ((0, 8),))
    stiff_terms = scatter_about(key_of[1], (TERMS, ENODES * NDOF, ENODES * NDOF), (ENODES * NDOF) ** -0.5, 1.25)
    reduced_coords = scatter_about(key_of[2], (MODES, SNAPS), 1.0, 6.0, ((1, 4),))
    sample_list = draw_sample_list(jax.random.fold_in(key_of[7], 71), 0)
    connectivity = draw_connectivity(jax.random.fold_in(key_of[7], 71), 0)
    node_slot = draw_node_slot(jax.random.fold_in(key_of[7], 71), 0)
    elem_device = draw_elem_device(jax.random.fold_in(key_of[7], 71), 0)
    return dict(node_basis=node_basis, stiff_terms=stiff_terms, reduced_coords=reduced_coords, sample_list=sample_list, connectivity=connectivity, node_slot=node_slot, elem_device=elem_device)


def count_slots(elem_device):
    position_ids = jnp.arange(elem_device.shape[0], dtype=jnp.int32)
    earlier = (position_ids[None, :] < position_ids[:, None]) & (elem_device[None, :] == elem_device[:, None])
    return jnp.sum(earlier.astype(jnp.int32), axis=1).astype(jnp.int32)

def reference(node_basis, stiff_terms, reduced_coords, sample_list, connectivity, node_slot, elem_device):
    sampled = EL_DEV * N_ELEM
    node_ids = connectivity[sample_list]
    live_nodes = node_ids >= 0
    stored_rows = jnp.where(live_nodes, node_slot[jnp.maximum(node_ids, 0)], 0).astype(jnp.int32)
    gathered = jnp.where(live_nodes[:, :, None], node_basis[stored_rows], jnp.zeros((), node_basis.dtype))
    local_basis = gathered.reshape(sampled, ENODES * NDOF, MODES)
    coords_wide = reduced_coords.astype(jnp.float32)
    terms_wide = stiff_terms.astype(jnp.float32)

    def project_one(element_basis):
        basis_wide = element_basis.astype(jnp.float32)
        displaced = jnp.einsum('km,ms->ks', basis_wide, coords_wide).astype(jnp.bfloat16)
        forces = jnp.einsum('tkl,ls->kst', terms_wide, displaced.astype(jnp.float32)).astype(jnp.bfloat16)
        forces = forces.reshape(ENODES * NDOF, COLS)
        return jnp.einsum('km,kc->mc', basis_wide, forces.astype(jnp.float32)).astype(jnp.bfloat16)
    projected = lax.map(project_one, local_basis)
    flat_rows = projected.reshape(sampled * MODES, COLS)
    gram_matrix = jnp.dot(flat_rows.T.astype(jnp.float32), flat_rows.astype(jnp.float32), preferred_element_type=jnp.float32) / (sampled * MODES)
    lower_factor = jnp.linalg.cholesky(gram_matrix)

    def solve_one(element_rows):
        return jax.scipy.linalg.solve_triangular(lower_factor, element_rows.astype(jnp.float32).T, lower=True).T
    live_panel = lax.map(solve_one, projected)
    slot_ids = count_slots(elem_device)
    ortho_panel = jnp.zeros((N_ELEM * CAP, MODES, COLS), jnp.float32).at[elem_device * CAP + slot_ids].set(live_panel)
    return (ortho_panel, lower_factor.T)
```

```python
import functools

import jax
import jax.numpy as jnp
from jax import lax
from jax.experimental import pallas as pl
from jax.experimental.pallas import tpu as pltpu
from jax.sharding import PartitionSpec as P

F32, BF16, I32 = jnp.float32, jnp.bfloat16, jnp.int32
NT = (((1,), (1,)), ((), ()))
NN = (((1,), (0,)), ((), ()))
LANES = 128
TILE = 256
BLOCK = 128
STEP = 8
VMEM_BYTES = 60 * 1024 * 1024
JOINED_LIMIT = 1 << 22


def dot(a, b, dims=NN):
    return lax.dot_general(a, b, dims, preferred_element_type=F32)


def split(x):
    high = x.astype(BF16)
    return high, (x - high.astype(F32)).astype(BF16)


def dot3(a, b, dims=NN):
    (ah, al), (bh, bl) = a, b
    return dot(ah, bh, dims) + (dot(ah, bl, dims) + dot(al, bh, dims))


def iota(shape, dim):
    return lax.broadcasted_iota(I32, shape, dim)


def quotient(x, n):
    return jnp.floor((x.astype(F32) + 0.5) * (1.0 / n)).astype(I32)


def node_places(sample, links, table):
    positions, elems = links.shape
    sampled = sample.shape[1]
    pick = (iota((elems, sampled), 0) == sample).astype(F32).astype(BF16)
    shifted = links + 1
    parts = jnp.concatenate([(shifted >> 8).astype(F32), (shifted & 255).astype(F32)], axis=0)
    found = dot(parts.astype(BF16), pick)
    nodes = (found[:positions] * 256.0 + found[positions:]).astype(I32) - 1
    halves = jnp.concatenate([(table >> 8).astype(F32), (table & 255).astype(F32)], axis=1).T.astype(BF16)
    high, low = jnp.maximum(nodes, 0) >> 7, jnp.maximum(nodes, 0) & (LANES - 1)
    places = jnp.zeros((positions, sampled), F32)
    for p in range(positions):
        rows = (iota((table.shape[0], sampled), 0) == high[p : p + 1]).astype(F32).astype(BF16)
        both = dot(halves, rows)
        here = iota((LANES, sampled), 0) == low[p : p + 1]
        value = both[:LANES] * 256.0 + both[LANES:]
        value = jnp.sum(jnp.where(here, value, 0.0), axis=0, keepdims=True)
        places = jnp.where(iota((positions, sampled), 0) == p, value, places)
    return jnp.where(nodes >= 0, places, -1.0)


def slot_picks(elem_device, device, capacity):
    sampled = elem_device.shape[1]
    mine = (elem_device == device).astype(F32)
    before = (iota((sampled, sampled), 0) < iota((sampled, sampled), 1)).astype(F32).astype(BF16)
    ranks = dot(jnp.broadcast_to(mine, (16, sampled)).astype(BF16), before)[0:1]
    return jnp.where(iota((capacity, sampled), 0).astype(F32) == ranks, mine, 0.0)


def owner_kernel(
    devices, groups, capacity, ndof, ids, sample, links, table, elem_device, basis, shared, slots, owners
):
    elem_rank, snap_rank = ids[0], ids[1]
    node_rows, width = basis.shape
    modes = width // ndof
    band = modes // groups
    sampled = sample.shape[1]
    quarter = sampled // groups
    first = slots.shape[1] - capacity
    places = node_places(sample[...], links[...], table[...])
    owner = jnp.floor((places + 0.5) * (1.0 / node_rows))
    owners[...] = jnp.where(places >= 0, owner, -1.0)
    here = (places >= 0) & (owner == elem_rank.astype(F32))
    local = places - (elem_rank * node_rows).astype(F32) + 1.0
    local = jnp.sum(jnp.where(here, local, 0.0), axis=0, keepdims=True)
    wanted = (iota((quarter, sampled), 1) == iota((quarter, sampled), 0) + snap_rank * quarter).astype(F32)
    picks = [wanted] + [slot_picks(elem_device[...], d, capacity) for d in range(devices)]
    row = jnp.sum(jnp.concatenate(picks, axis=0) * local, axis=1, keepdims=True).astype(I32) - 1
    one_hot = (iota((row.shape[0], node_rows), 1) == row).astype(F32).astype(BF16)
    for c in range(ndof):
        rows = dot(one_hot, basis[:, c * modes : (c + 1) * modes])
        full = rows[:quarter].astype(BF16)
        part = jnp.zeros((devices * capacity, band), F32)
        for k in range(groups):
            part = jnp.where(snap_rank == k, rows[quarter:, k * band : (k + 1) * band], part)
        part = part.astype(BF16)
        for d in range(shared.shape[0]):
            shared[d, c * quarter : (c + 1) * quarter, :] = full
        for d in range(devices):
            slots[d, first:, c * band : (c + 1) * band] = part[d * capacity : (d + 1) * capacity]
    for d in range(devices):
        slots[d, first:, ndof * band :] = jnp.zeros((capacity, modes - ndof * band), BF16)


def owner_kernel_joined(devices, groups, capacity, ndof, *refs):
    owner_kernel(devices, groups, capacity, ndof, *refs[:-2], refs[-2], refs[-2], refs[-1])


def place_one_hot(owner_col, lane_count, ndof, pitch, live, members):
    rows = owner_col.shape[0]
    index = iota((rows, 1), 0)
    member, row = index // pitch, index % pitch
    position = quotient(row, ndof)
    dof = row - position * ndof
    target = (owner_col.astype(I32) * ndof + dof) * members + member
    target = jnp.where((owner_col >= 0) & (row < live), target, -1)
    return (iota((rows, lane_count), 1) == target).astype(F32).astype(BF16)


def owner_rows(owners, rows, ndof, pitch):
    positions = owners.shape[0]
    position = quotient(iota((rows, positions), 0) % pitch, ndof)
    pick = (position == iota((rows, positions), 1)).astype(F32).astype(BF16)
    return dot(pick, owners.astype(BF16))


def element_kernel(ndof, pitch, ids, got, coords, owners, out):
    snap_rank = ids[1]
    devices, _, modes = got.shape
    positions, sampled = owners.shape
    members = 16
    live = positions * ndof
    quarter = out.shape[1] // pitch
    snaps = out.shape[0] - 2 * pitch
    per_tile = TILE // pitch
    rows = members * pitch
    own = owner_rows(owners[...], rows, ndof, pitch)
    for h in range(quarter // members):
        first = snap_rank * quarter + h * members
        at = iota((rows, sampled), 1) == iota((rows, sampled), 0) // pitch + first
        owner_col = jnp.sum(jnp.where(at, own, 0.0), axis=1, keepdims=True)
        source = jnp.concatenate(
            [
                got[o, c * quarter + h * members : c * quarter + (h + 1) * members, :]
                for o in range(devices)
                for c in range(ndof)
            ],
            axis=0,
        )
        basis = dot(place_one_hot(owner_col, source.shape[0], ndof, pitch, live, members), source).astype(BF16)
        moved = dot(coords[...], basis, NT).astype(BF16)
        out[0:snaps, h * rows : (h + 1) * rows] = moved
        for g in range(rows // TILE):
            part = basis[g * TILE : (g + 1) * TILE]
            square = dot(part, part, NT)
            block = jnp.zeros((pitch, TILE), F32)
            for i in range(per_tile):
                inside = iota((pitch, TILE), 1) // pitch == i
                block = jnp.where(inside, square[i * pitch : (i + 1) * pitch], block)
            high, low = split(block)
            lanes = slice(h * rows + g * TILE, h * rows + (g + 1) * TILE)
            out[snaps : snaps + pitch, lanes] = high
            out[snaps + pitch :, lanes] = low


def spread(x):
    return jnp.broadcast_to(x, (STEP, LANES))


def factor_block(block):
    count = BLOCK // STEP
    left = [block[STEP * c : STEP * c + STEP] for c in range(count)]
    right = [
        (iota((STEP, LANES), 1) == iota((STEP, LANES), 0) + STEP * c).astype(F32)
        for c in range(count)
    ]
    sub = iota((STEP, LANES), 0)
    upper, inverse = [], []
    for j in range(count):
        base = STEP * j
        s = {
            (i, k): spread(left[j][i : i + 1, base + k : base + k + 1])
            for k in range(STEP)
            for i in range(k, STEP)
        }
        ul = [spread(left[j][k : k + 1]) for k in range(STEP)]
        ur = [spread(right[j][k : k + 1]) for k in range(STEP)]
        scale, low = [], {}
        out_l, out_r = jnp.zeros((STEP, LANES), F32), jnp.zeros((STEP, LANES), F32)
        for k in range(STEP):
            root = lax.rsqrt(s[k, k])
            scale.append(root)
            for i in range(k + 1, STEP):
                low[i, k] = s[i, k] * root
            for m in range(k + 1, STEP):
                for i in range(m, STEP):
                    s[i, m] = s[i, m] - low[i, k] * low[m, k]
            ul[k], ur[k] = ul[k] * root, ur[k] * root
            for i in range(k + 1, STEP):
                ul[i] = ul[i] - low[i, k] * ul[k]
                ur[i] = ur[i] - low[i, k] * ur[k]
            out_l = jnp.where(sub == k, ul[k], out_l)
            out_r = jnp.where(sub == k, ur[k], out_r)
        keep = iota((STEP, LANES), 1) >= sub + base
        upper.append(jnp.where(keep, out_l, 0.0))
        inverse.append(out_r)
        for c in range(j + 1, count):
            column = [spread(left[c][:, base + k : base + k + 1]) for k in range(STEP)]
            for k in range(STEP):
                m = column[k] * scale[k]
                for i in range(k + 1, STEP):
                    column[i] = column[i] - m * low[i, k]
                left[c] = left[c] - m * ul[k]
                right[c] = right[c] - m * ur[k]
    return jnp.concatenate(upper, axis=0), jnp.concatenate(inverse, axis=0)


def panel_kernel(
    ndof, pitch, total_rows, ids, every, got, owners, elem_device, stiff, panel, factor, forces, halves, work, upper
):
    elem_rank = ids[0]
    groups, height, lanes = every.shape
    snaps = height - 2 * pitch
    terms, live, _ = stiff.shape
    columns = snaps * terms
    capacity, band, _ = panel.shape
    devices = got.shape[0]
    positions, sampled = owners.shape
    per_tile = TILE // pitch
    tiles = [(q, t) for q in range(groups) for t in range(lanes // TILE)]
    slot_rows = capacity * pitch
    slot_tiles = slot_rows // TILE
    chunk = 8

    picks = slot_picks(elem_device[...], elem_rank, capacity)
    member = iota((slot_rows, capacity), 0) // pitch
    expand = (member == iota((slot_rows, capacity), 1)).astype(F32).astype(BF16)
    picks = dot(expand, picks.astype(BF16))
    own = owner_rows(owners[...], slot_rows, ndof, pitch)
    owner_col = jnp.sum(picks * (own + 1.0), axis=1, keepdims=True) - 1.0
    which = jnp.sum(picks * (iota((slot_rows, sampled), 1) + 1).astype(F32), axis=1, keepdims=True).astype(I32) - 1
    first = got.shape[1] - capacity
    source = jnp.concatenate(
        [got[o, first:, c * band : (c + 1) * band] for o in range(devices) for c in range(ndof)], axis=0
    )
    basis = dot(place_one_hot(owner_col, source.shape[0], ndof, pitch, live, capacity), source)
    basis_t = basis.T

    lane = which * pitch + iota((slot_rows, 1), 0) % pitch
    lane = jnp.where(which >= 0, lane, -1)
    slot_moved = jnp.zeros((snaps, slot_rows), F32)
    for n, (q, t) in enumerate(tiles):
        pick = (iota((slot_rows, TILE), 1) + n * TILE == lane).astype(F32).astype(BF16)
        slot_moved = slot_moved + dot(every[q, 0:snaps, t * TILE : (t + 1) * TILE], pick, NT)
    slot_moved = slot_moved.astype(BF16)

    tile_of = (iota((live, TILE), 1) % pitch == iota((live, TILE), 0)).astype(F32).astype(BF16)
    diagonal = iota((TILE, TILE), 0) // pitch == iota((TILE, TILE), 1) // pitch
    terms_wide = []
    for t in range(terms):
        wide = dot(stiff[t], tile_of)
        wide = jnp.concatenate([wide, jnp.zeros((pitch - live, TILE), F32)], axis=0)
        wide = jnp.concatenate([wide] * per_tile, axis=0)
        terms_wide.append(jnp.where(diagonal, wide, 0.0).astype(BF16))

    gram = None
    for start in range(0, len(tiles), chunk):
        part = tiles[start : start + chunk]
        moved = [every[q, 0:snaps, t * TILE : (t + 1) * TILE] for q, t in part]
        if start == 0:
            moved += [slot_moved[:, t * TILE : (t + 1) * TILE] for t in range(slot_tiles)]
        moved = jnp.concatenate(moved, axis=0)
        for t in range(terms):
            force = dot(moved, terms_wide[t], NT)
            for n in range(moved.shape[0] // snaps):
                for h in range(TILE // LANES):
                    piece = force[n * snaps : (n + 1) * snaps, h * LANES : (h + 1) * LANES]
                    forces[n * TILE // LANES + h, pl.ds(t, snaps, stride=terms), :] = piece
        if start == 0:
            for h in range(slot_rows // LANES):
                piece = forces[len(part) * TILE // LANES + h].astype(BF16).astype(F32)
                work[:, columns + h * LANES : columns + (h + 1) * LANES] = piece
        for n, (q, t) in enumerate(part):
            force = [forces[n * TILE // LANES + h] for h in range(TILE // LANES)]
            force = jnp.concatenate(force, axis=1).astype(BF16)
            cut = slice(t * TILE, (t + 1) * TILE)
            total = None
            for low in (0, 1):
                rows = every[q, snaps + low * pitch : snaps + (low + 1) * pitch, cut].astype(F32)
                wide = jnp.concatenate([rows] * per_tile, axis=0)
                term = dot(force, jnp.where(diagonal, wide, 0.0).astype(BF16))
                total = term if total is None else total + term
            halves[0, :, n * TILE : (n + 1) * TILE] = force
            halves[1, :, n * TILE : (n + 1) * TILE], halves[2, :, n * TILE : (n + 1) * TILE] = split(total)
        end = len(part) * TILE
        term = dot(halves[0, :, :end], halves[1, :, :end], NT) + dot(halves[0, :, :end], halves[2, :, :end], NT)
        gram = term if gram is None else gram + term
    work[:, :columns] = gram * (1.0 / total_rows)

    for b in range(columns // BLOCK):
        here = slice(b * BLOCK, (b + 1) * BLOCK)
        after = (b + 1) * BLOCK
        top, inverse = factor_block(work[here, here])
        upper[here, here] = top
        if b:
            upper[here, : b * BLOCK] = jnp.zeros((BLOCK, b * BLOCK), F32)
        inverse = split(inverse)
        across = dot3(inverse, split(work[here, after:]))
        work[here, after:] = across
        if after < columns:
            upper[here, after:] = across[:, : columns - after]
            down = dot3(split(work[after:columns, here]), inverse, NT)
            work[after:columns, after:] = work[after:columns, after:] - dot3(split(down), split(across))

    share = factor.shape[0]
    factor[...] = upper[pl.ds(pl.multiple_of(elem_rank * share, share), share), :]

    each = LANES // pitch
    for n in range(slot_rows // LANES):
        cut = slice(columns + n * LANES, columns + (n + 1) * LANES)
        high, low = split(work[:, cut])
        right = jnp.concatenate([high, low], axis=1)
        rows = basis_t[:, n * LANES : (n + 1) * LANES]
        left = jnp.concatenate(
            [jnp.where(iota((band, LANES), 1) // pitch == i, rows, 0.0) for i in range(each)], axis=0
        ).astype(BF16)
        result = dot(jnp.concatenate([left, left], axis=1), right, NT)
        for i in range(each):
            panel[n * each + i] = result[i * band : (i + 1) * band]


def shards(node_basis, stiff_terms, reduced_coords, sample_list, connectivity, node_slot, elem_device):
    devices = lax.axis_size("elem")
    groups = lax.axis_size("snap")
    node_rows, width = node_basis.shape
    modes, local_snaps = reduced_coords.shape
    snaps = local_snaps * groups
    ndof = width // modes
    terms, live, _ = stiff_terms.shape
    sampled = sample_list.shape[0]
    positions = connectivity.shape[1]
    capacity = 2 * sampled // devices
    quarter = sampled // groups
    pitch = 32
    band = modes // groups
    columns = snaps * terms
    total_rows = sampled * modes
    chunk_lanes = min(sampled * pitch, 8 * TILE)
    slot_rows = capacity * pitch

    ids = jnp.stack([lax.axis_index("elem"), lax.axis_index("snap")]).astype(I32)
    smem = pl.BlockSpec(memory_space=pltpu.SMEM)
    vmem = pl.BlockSpec(memory_space=pltpu.VMEM)
    params = pltpu.CompilerParams(vmem_limit_bytes=VMEM_BYTES)

    coords = lax.all_gather(reduced_coords.T, "snap", axis=0, tiled=True)
    sample_row = sample_list.reshape(1, sampled)
    device_row = elem_device.reshape(1, sampled)
    table = node_slot.reshape(-1, LANES)
    shared_rows = ndof * quarter
    joined = devices * (shared_rows + capacity) * modes <= JOINED_LIMIT
    if joined:
        sent = ((devices, shared_rows + capacity, modes),)
    else:
        sent = ((1, shared_rows, modes), (devices, capacity, modes))
    *sent, owners = pl.pallas_call(
        functools.partial(owner_kernel_joined if joined else owner_kernel, devices, groups, capacity, ndof),
        out_shape=tuple(jax.ShapeDtypeStruct(shape, BF16) for shape in sent)
        + (jax.ShapeDtypeStruct((positions, sampled), F32),),
        in_specs=[smem] + [vmem] * 5,
        out_specs=(vmem,) * (len(sent) + 1),
        compiler_params=params,
        name="owner_rows",
    )(ids, sample_row, connectivity.T, table, device_row, node_basis)
    slots = lax.all_to_all(sent[-1], "elem", split_axis=0, concat_axis=0, tiled=True)
    got = slots if joined else lax.all_gather(sent[0], "elem", axis=0, tiled=True)

    mine = pl.pallas_call(
        functools.partial(element_kernel, ndof, pitch),
        out_shape=jax.ShapeDtypeStruct((snaps + 2 * pitch, quarter * pitch), BF16),
        in_specs=[smem] + [vmem] * 3,
        out_specs=vmem,
        compiler_params=params,
        name="element_squares",
    )(ids, got, coords, owners)
    every = lax.all_gather(mine, "snap", axis=0)

    return pl.pallas_call(
        functools.partial(panel_kernel, ndof, pitch, total_rows),
        out_shape=(
            jax.ShapeDtypeStruct((capacity, band, columns), F32),
            jax.ShapeDtypeStruct((columns // devices, columns), F32),
        ),
        in_specs=[smem] + [vmem] * 5,
        out_specs=(vmem, vmem),
        scratch_shapes=[
            pltpu.VMEM(((chunk_lanes + slot_rows) // LANES, columns, LANES), F32),
            pltpu.VMEM((3, columns, chunk_lanes), BF16),
            pltpu.VMEM((columns, columns + slot_rows), F32),
            pltpu.VMEM((columns, columns), F32),
        ],
        compiler_params=params,
        name="panel",
    )(ids, every, slots, owners, device_row, stiff_terms)


def solution(mesh):
    placed = (P("elem", None), P(), P(None, "snap"), P(), P(), P(), P())
    return jax.shard_map(
        shards,
        mesh=mesh,
        in_specs=placed,
        out_specs=(P("elem", "snap", None), P("elem", None)),
        check_vma=False,
    )
```

```python
import functools

import jax
import jax.numpy as jnp
from jax import lax
from jax.experimental import pallas as pl
from jax.experimental.pallas import tpu as pltpu
from jax.sharding import PartitionSpec as P

F32, BF16, I32 = jnp.float32, jnp.bfloat16, jnp.int32
NT = (((1,), (1,)), ((), ()))
NN = (((1,), (0,)), ((), ()))
TN = (((0,), (0,)), ((), ()))
LANES = 128
TILE = 256
BLOCK = 128
PANEL = 64
STEP = 8
MEBI = 1 << 20
JOINED_LIMIT = 1 << 22
ROWS_PER_TABLE = 512


def dot(a, b, dims=NN):
    return lax.dot_general(a, b, dims, preferred_element_type=F32)


def split(x):
    high = x.astype(BF16)
    return high, (x - high.astype(F32)).astype(BF16)


def dot3(a, b, dims=NN):
    (ah, al), (bh, bl) = a, b
    return dot(ah, bh, dims) + (dot(ah, bl, dims) + dot(al, bh, dims))


def iota(shape, dim):
    return lax.broadcasted_iota(I32, shape, dim)


def quotient(x, n):
    return jnp.floor((x.astype(F32) + 0.5) * (1.0 / n)).astype(I32)


def node_places(sample, links, table):
    positions, elems = links.shape
    sampled = sample.shape[1]
    pick = (iota((elems, sampled), 0) == sample).astype(F32).astype(BF16)
    shifted = links + 1
    parts = jnp.concatenate([(shifted >> 8).astype(F32), (shifted & 255).astype(F32)], axis=0)
    found = dot(parts.astype(BF16), pick)
    nodes = (found[:positions] * 256.0 + found[positions:]).astype(I32) - 1
    halves = jnp.concatenate([(table >> 8).astype(F32), (table & 255).astype(F32)], axis=1).T.astype(BF16)
    high, low = jnp.maximum(nodes, 0) >> 7, jnp.maximum(nodes, 0) & (LANES - 1)
    places = jnp.zeros((positions, sampled), F32)
    for p in range(positions):
        rows = (iota((table.shape[0], sampled), 0) == high[p : p + 1]).astype(F32).astype(BF16)
        both = dot(halves, rows)
        here = iota((LANES, sampled), 0) == low[p : p + 1]
        value = both[:LANES] * 256.0 + both[LANES:]
        value = jnp.sum(jnp.where(here, value, 0.0), axis=0, keepdims=True)
        places = jnp.where(iota((positions, sampled), 0) == p, value, places)
    return jnp.where(nodes >= 0, places, -1.0)


def slot_picks(elem_device, device, capacity):
    sampled = elem_device.shape[1]
    mine = (elem_device == device).astype(F32)
    before = (iota((sampled, sampled), 0) < iota((sampled, sampled), 1)).astype(F32).astype(BF16)
    ranks = dot(jnp.broadcast_to(mine, (16, sampled)).astype(BF16), before)[0:1]
    return jnp.where(iota((capacity, sampled), 0).astype(F32) == ranks, mine, 0.0)


def owner_kernel(devices, groups, capacity, ndof, *refs):
    inputs, outputs = refs[:5], refs[5:-6]
    *held, basis, sems = refs[-6:]
    shared, slots, owners = outputs[0], outputs[-2], outputs[-1]
    sample, links, table, elem_device = held[:4]
    modes = basis.shape[1] // ndof
    copies = [pltpu.make_async_copy(ref, to, sems.at[n]) for n, (ref, to) in enumerate(zip(inputs[:4], held))]
    for c in range(ndof):
        part = slice(c * modes, (c + 1) * modes)
        copies.append(pltpu.make_async_copy(inputs[4].at[:, part], basis.at[:, part], sems.at[4 + c]))
    for copy in copies:
        copy.start()
    elem_rank, snap_rank = lax.axis_index("elem"), lax.axis_index("snap")
    node_rows = basis.shape[0]
    band = modes // groups
    sampled = sample.shape[1]
    quarter = sampled // groups
    first = slots.shape[1] - capacity
    for copy in copies[:4]:
        copy.wait()
    places = node_places(sample[...], links[...], table[...])
    owner = jnp.floor((places + 0.5) * (1.0 / node_rows))
    owners[...] = jnp.where(places >= 0, owner, -1.0)
    here = (places >= 0) & (owner == elem_rank.astype(F32))
    local = places - (elem_rank * node_rows).astype(F32) + 1.0
    local = jnp.sum(jnp.where(here, local, 0.0), axis=0, keepdims=True)
    wanted = (iota((quarter, sampled), 1) == iota((quarter, sampled), 0) + snap_rank * quarter).astype(F32)
    picks = [wanted] + [slot_picks(elem_device[...], d, capacity) for d in range(devices)]
    row = jnp.sum(jnp.concatenate(picks, axis=0) * local, axis=1, keepdims=True).astype(I32) - 1
    pick = (iota((row.shape[0], node_rows), 1) == row).astype(F32).astype(BF16)
    for c in range(ndof):
        copies[4 + c].wait()
        rows = dot(pick, basis[:, c * modes : (c + 1) * modes])
        full = rows[:quarter].astype(BF16)
        part = jnp.zeros((devices * capacity, band), F32)
        for k in range(groups):
            part = jnp.where(snap_rank == k, rows[quarter:, k * band : (k + 1) * band], part)
        part = part.astype(BF16)
        for d in range(shared.shape[0]):
            shared[d, c * quarter : (c + 1) * quarter, :] = full
        for d in range(devices):
            slots[d, first:, c * band : (c + 1) * band] = part[d * capacity : (d + 1) * capacity]
    for d in range(devices):
        slots[d, first:, ndof * band :] = jnp.zeros((capacity, modes - ndof * band), BF16)


def place_targets(owner_col, ndof, pitch, live, members):
    index = iota(owner_col.shape, 0)
    member, row = index // pitch, index % pitch
    position = quotient(row, ndof)
    dof = row - position * ndof
    target = (owner_col.astype(I32) * ndof + dof) * members + member
    target = jnp.where((owner_col >= 0) & (row < live), target, -1)
    return jnp.broadcast_to(target, (owner_col.shape[0], LANES))


def one_hot(targets, lane_count, start=0):
    rows = targets.shape[0]
    wide = [iota((rows, LANES), 1) + (start + at) == targets for at in range(0, lane_count, LANES)]
    return jnp.concatenate([w.astype(F32).astype(BF16) for w in wide], axis=1)


def owner_rows(owners, rows, ndof, pitch):
    positions = owners.shape[0]
    position = quotient(iota((rows, positions), 0) % pitch, ndof)
    pick = (position == iota((rows, positions), 1)).astype(F32).astype(BF16)
    return dot(pick, owners.astype(BF16))


def table_kernel(ndof, pitch, groups, owners, elem_device, quarter_places, slot_places, slot_lane):
    elem_rank, snap_rank = lax.axis_index("elem"), lax.axis_index("snap")
    positions, sampled = owners.shape
    live = positions * ndof
    quarter = sampled // groups
    parts, rows, _ = quarter_places.shape
    members = rows // pitch
    own = owner_rows(owners[...], rows, ndof, pitch)
    for h in range(parts):
        first = snap_rank * quarter + h * members
        at = iota((rows, sampled), 1) == iota((rows, sampled), 0) // pitch + first
        owner_col = jnp.sum(jnp.where(at, own, 0.0), axis=1, keepdims=True)
        quarter_places[h] = place_targets(owner_col, ndof, pitch, live, members)

    rows = slot_places.shape[0]
    capacity = rows // pitch
    picks = slot_picks(elem_device[...], elem_rank, capacity)
    member = iota((rows, capacity), 0) // pitch
    expand = (member == iota((rows, capacity), 1)).astype(F32).astype(BF16)
    picks = dot(expand, picks.astype(BF16))
    own = owner_rows(owners[...], rows, ndof, pitch)
    owner_col = jnp.sum(picks * (own + 1.0), axis=1, keepdims=True) - 1.0
    slot_places[...] = place_targets(owner_col, ndof, pitch, live, capacity)
    which = jnp.sum(picks * (iota((rows, sampled), 1) + 1).astype(F32), axis=1, keepdims=True).astype(I32) - 1
    lane = which * pitch + iota((rows, 1), 0) % pitch
    slot_lane[...] = jnp.broadcast_to(jnp.where(which >= 0, lane, -1), (rows, LANES))


def element_kernel(ndof, pitch, got, coords, places, out):
    devices = got.shape[0]
    parts, rows, _ = places.shape
    members = rows // pitch
    quarter = parts * members
    snaps = out.shape[0] - 2 * pitch
    per_tile = TILE // pitch
    for h in range(parts):
        source = jnp.concatenate(
            [
                got[o, c * quarter + h * members : c * quarter + (h + 1) * members, :]
                for o in range(devices)
                for c in range(ndof)
            ],
            axis=0,
        )
        basis = dot(one_hot(places[h], source.shape[0]), source).astype(BF16)
        moved = dot(coords[...], basis, NT).astype(BF16)
        out[0:snaps, h * rows : (h + 1) * rows] = moved
        for g in range(rows // TILE):
            part = basis[g * TILE : (g + 1) * TILE]
            square = dot(part, part, NT)
            block = jnp.zeros((pitch, TILE), F32)
            for i in range(per_tile):
                inside = iota((pitch, TILE), 1) // pitch == i
                block = jnp.where(inside, square[i * pitch : (i + 1) * pitch], block)
            high, low = split(block)
            lanes = slice(h * rows + g * TILE, h * rows + (g + 1) * TILE)
            out[snaps : snaps + pitch, lanes] = high
            out[snaps + pitch :, lanes] = low


def spread(x):
    return jnp.broadcast_to(x, (STEP, LANES))


def factor_block(block, rows, work):
    count, per = BLOCK // STEP, PANEL // STEP
    span = range(STEP)
    left = [block[STEP * c : STEP * c + STEP] for c in range(count)]
    right = [
        (iota((STEP, LANES), 1) == iota((STEP, LANES), 0) + STEP * c).astype(F32) for c in range(count)
    ]
    sub = iota((STEP, LANES), 0)

    def columns_of(c, base):
        return [spread(left[c][:, base + k : base + k + 1]) for k in span]

    upper, inverse = [], []
    work = list(work)
    own = near = None
    for j in range(count):
        base = STEP * j
        end = (j // per + 1) * per
        rows[j, 0], rows[j, 1] = left[j], right[j]
        ul = [spread(rows[j, 0, k : k + 1]) for k in span]
        ur = [spread(rows[j, 1, k : k + 1]) for k in span]
        own = columns_of(j, base) if own is None else own
        for k in span:
            rows[j, 2 + k] = own[k]
        s = {(i, k): spread(rows[j, 2 + k, i : i + 1]) for k in span for i in range(k, STEP)}
        below = {c: columns_of(c, base) for c in range(j + 1, end)}
        if near is not None:
            below[j + 1] = near
        next_own = columns_of(j + 1, base + STEP) if j + 1 < end else None
        next_near = columns_of(j + 2, base + STEP) if j + 2 < end else None
        low = {}
        out_l, out_r = jnp.zeros((STEP, LANES), F32), jnp.zeros((STEP, LANES), F32)
        for k in span:
            root = lax.rsqrt(s[k, k])
            for i in range(k + 1, STEP):
                low[i, k] = s[i, k] * root
            for m in range(k + 1, STEP):
                for i in range(m, STEP):
                    s[i, m] = s[i, m] - low[i, k] * low[m, k]
            ul[k], ur[k] = ul[k] * root, ur[k] * root
            for i in range(k + 1, STEP):
                ul[i] = ul[i] - low[i, k] * ul[k]
                ur[i] = ur[i] - low[i, k] * ur[k]
            out_l = jnp.where(sub == k, ul[k], out_l)
            out_r = jnp.where(sub == k, ur[k], out_r)
            scaled = {}
            for c, col in below.items():
                scaled[c] = col[k] * root
                for i in range(k + 1, STEP):
                    col[i] = col[i] - scaled[c] * low[i, k]
                left[c] = left[c] - scaled[c] * ul[k]
                right[c] = right[c] - scaled[c] * ur[k]
            if next_own is not None:
                rows[j, 2 + STEP + k] = scaled[j + 1]
                for i in span:
                    other = spread(rows[j, 2 + STEP + k, i : i + 1])
                    next_own[i] = next_own[i] - scaled[j + 1] * other
                    if next_near is not None:
                        next_near[i] = next_near[i] - scaled[j + 2] * other
        own, near = next_own, next_near
        keep = iota((STEP, LANES), 1) >= sub + base
        upper.append(jnp.where(keep, out_l, 0.0))
        inverse.append(out_r)
        if j + 1 == end and end < count:
            lh, ll = split(jnp.concatenate(upper[end - per : end], axis=0))
            rh, rl = split(jnp.concatenate(inverse[end - per : end], axis=0))
            both_h, both_l = jnp.concatenate([lh, rh], axis=1), jnp.concatenate([ll, rl], axis=1)
            update = dot(
                jnp.concatenate([lh, lh, ll], axis=0), jnp.concatenate([both_h, both_l, both_h], axis=0), TN
            )
            for c in range(end, count):
                left[c] = left[c] - update[STEP * c : STEP * c + STEP, :LANES]
                right[c] = right[c] - update[STEP * c : STEP * c + STEP, LANES:]
        for _ in range(-(-len(work) // (count - j))):
            work.pop(0)()
    return jnp.concatenate(upper, axis=0), jnp.concatenate(inverse, axis=0)


def cut(b):
    return slice(b * BLOCK, (b + 1) * BLOCK)


def factorize(gram, side, lower, rows):
    count = gram.shape[0] // BLOCK
    block, work = gram[cut(0), cut(0)], []
    for b in range(count):
        top, inverse = factor_block(block, rows.at[b % 2], work)
        lower[cut(b), cut(b)] = top.T
        inverse, down, across, work = split(inverse), {}, {}, []

        def below(r, b=b, inverse=inverse, down=down):
            value = dot3(split(gram[cut(r), cut(b)]), inverse, NT)
            lower[cut(r), cut(b)] = value
            down[r] = split(value)

        def update(r, c, down=down):
            gram[cut(r), cut(c)] = gram[cut(r), cut(c)] - dot3(down[r], down[c], NT)

        def solve(h, b=b, inverse=inverse, across=across):
            value = dot3(inverse, split(side[cut(b), h : h + TILE]))
            side[cut(b), h : h + TILE] = value
            across[h] = split(value)

        def reduce(r, h, down=down, across=across):
            side[cut(r), h : h + TILE] = side[cut(r), h : h + TILE] - dot3(down[r], across[h])

        if b + 1 < count:
            below(b + 1)
            block = gram[cut(b + 1), cut(b + 1)] - dot3(down[b + 1], down[b + 1], NT)
        work = [functools.partial(below, r) for r in range(b + 2, count)]
        work += [functools.partial(update, r, c) for r in range(b + 2, count) for c in range(b + 1, r + 1)]
        for h in range(0, side.shape[1], TILE):
            work.append(functools.partial(solve, h))
            work += [functools.partial(reduce, r, h) for r in range(b + 1, count)]
    for step in work:
        step()


def panel_kernel(
    ndof, pitch, total_rows, every, got, places, slot_lane, stiff, panel, factor, forces, halves, gram, side,
    lower, turned, rows, result, sems,
):
    elem_rank = lax.axis_index("elem")
    groups, height, lanes = every.shape
    snaps = height - 2 * pitch
    terms, live, _ = stiff.shape
    columns = snaps * terms
    capacity, band, _ = panel.shape
    devices = got.shape[0]
    per_tile = TILE // pitch
    tiles = [(q, t) for q in range(groups) for t in range(lanes // TILE)]
    slot_rows = capacity * pitch
    slot_tiles = slot_rows // TILE
    chunk = 8

    first = got.shape[1] - capacity
    source = jnp.concatenate(
        [got[o, first:, c * band : (c + 1) * band] for o in range(devices) for c in range(ndof)], axis=0
    )
    basis_t = dot(one_hot(places[...], source.shape[0]), source).T

    slot_moved = jnp.zeros((snaps, slot_rows), F32)
    for n, (q, t) in enumerate(tiles):
        pick = one_hot(slot_lane[...], TILE, n * TILE)
        slot_moved = slot_moved + dot(every[q, 0:snaps, t * TILE : (t + 1) * TILE], pick, NT)
    slot_moved = slot_moved.astype(BF16)

    tile_of = (iota((live, TILE), 1) % pitch == iota((live, TILE), 0)).astype(F32).astype(BF16)
    diagonal = iota((TILE, TILE), 0) // pitch == iota((TILE, TILE), 1) // pitch
    terms_wide = []
    for t in range(terms):
        wide = dot(stiff[t], tile_of)
        wide = jnp.concatenate([wide, jnp.zeros((pitch - live, TILE), F32)], axis=0)
        wide = jnp.concatenate([wide] * per_tile, axis=0)
        terms_wide.append(jnp.where(diagonal, wide, 0.0).astype(BF16))

    def add_chunk(tiles, slot_part):
        def piece_of(q, t, first, count):
            return every[q, first : first + count, pl.ds(pl.multiple_of(t * TILE, TILE), TILE)]

        moved = [piece_of(q, t, 0, snaps) for q, t in tiles] + slot_part
        moved = jnp.concatenate(moved, axis=0)
        for t in range(terms):
            force = dot(moved, terms_wide[t], NT)
            for n in range(moved.shape[0] // snaps):
                for h in range(TILE // LANES):
                    piece = force[n * snaps : (n + 1) * snaps, h * LANES : (h + 1) * LANES]
                    forces[n * TILE // LANES + h, pl.ds(t, snaps, stride=terms), :] = piece
        end = len(tiles) * TILE
        for h in range(len(slot_part) * TILE // LANES):
            side[:, h * LANES : (h + 1) * LANES] = forces[end // LANES + h].astype(BF16).astype(F32)
        for n, (q, t) in enumerate(tiles):
            force = [forces[n * TILE // LANES + h] for h in range(TILE // LANES)]
            force = jnp.concatenate(force, axis=1).astype(BF16)
            total = None
            for low in (0, 1):
                square = piece_of(q, t, snaps + low * pitch, pitch)
                wide = jnp.concatenate([square.astype(F32)] * per_tile, axis=0)
                term = dot(force, jnp.where(diagonal, wide, 0.0).astype(BF16))
                total = term if total is None else total + term
            halves[0, :, n * TILE : (n + 1) * TILE] = force
            halves[1, :, n * TILE : (n + 1) * TILE], halves[2, :, n * TILE : (n + 1) * TILE] = split(total)
        for b in range(columns // BLOCK):
            upto = (b + 1) * BLOCK
            term = dot(halves[0, cut(b), :end], halves[1, :upto, :end], NT)
            term = term + dot(halves[0, cut(b), :end], halves[2, :upto, :end], NT)
            term = term * (1.0 / total_rows)
            gram[cut(b), :upto] = term if slot_part else gram[cut(b), :upto] + term

    add_chunk(tiles[:chunk], [slot_moved[:, t * TILE : (t + 1) * TILE] for t in range(slot_tiles)])
    per_group = lanes // TILE
    if len(tiles) > chunk:

        @pl.loop(1, len(tiles) // chunk)
        def _(step):
            numbers = [step * chunk + n for n in range(chunk)]
            add_chunk([(n // per_group, n % per_group) for n in numbers], [])

    for b in range(columns // BLOCK):
        for c in range(b):
            lower[cut(c), cut(b)] = jnp.zeros((BLOCK, BLOCK), F32)
    factorize(gram, side, lower, rows)

    share = factor.shape[0]
    block = elem_rank * share // BLOCK
    columns_here = lower[:, pl.ds(pl.multiple_of(block * BLOCK, BLOCK), BLOCK)]
    turned[...] = columns_here.T
    factor[...] = turned[pl.ds(pl.multiple_of(elem_rank * share - block * BLOCK, share), share), :]

    each = LANES // pitch
    copies = []
    for n in range(slot_rows // LANES):
        high, low = split(side[:, n * LANES : (n + 1) * LANES])
        right = jnp.concatenate([high, low], axis=1)
        piece = basis_t[:, n * LANES : (n + 1) * LANES]
        left = jnp.concatenate(
            [jnp.where(iota((band, LANES), 1) // pitch == i, piece, 0.0) for i in range(each)], axis=0
        ).astype(BF16)
        values = dot(jnp.concatenate([left, left], axis=1), right, NT)
        for i in range(each):
            result[n * each + i] = values[i * band : (i + 1) * band]
        here = pl.ds(n * each, each)
        copies.append(pltpu.make_async_copy(result.at[here], panel.at[here], sems.at[n]))
        copies[-1].start()
    for copy in copies:
        copy.wait()


def room(mebi, *arrays):
    size = sum(2 * a.size * a.dtype.itemsize for a in arrays)
    return pltpu.CompilerParams(vmem_limit_bytes=min(60 * MEBI, mebi * MEBI + size))


def shards(node_basis, stiff_terms, reduced_coords, sample_list, connectivity, node_slot, elem_device):
    devices = lax.axis_size("elem")
    groups = lax.axis_size("snap")
    node_rows, width = node_basis.shape
    modes, local_snaps = reduced_coords.shape
    snaps = local_snaps * groups
    ndof = width // modes
    terms, live, _ = stiff_terms.shape
    sampled = sample_list.shape[0]
    positions = connectivity.shape[1]
    capacity = 2 * sampled // devices
    quarter = sampled // groups
    pitch = 32
    band = modes // groups
    columns = snaps * terms
    total_rows = sampled * modes
    chunk_lanes = min(sampled * pitch, 8 * TILE)
    slot_rows = capacity * pitch

    vmem = pl.BlockSpec(memory_space=pltpu.VMEM)

    coords = lax.all_gather(reduced_coords.T, "snap", axis=0, tiled=True)
    sample_row = sample_list.reshape(1, sampled)
    device_row = elem_device.reshape(1, sampled)
    table = node_slot.reshape(-1, LANES)
    shared_rows = ndof * quarter
    joined = devices * (shared_rows + capacity) * modes <= JOINED_LIMIT
    if joined:
        sent = ((devices, shared_rows + capacity, modes),)
    else:
        sent = ((1, shared_rows, modes), (devices, capacity, modes))
    wanted = [jax.ShapeDtypeStruct(shape, BF16) for shape in sent]
    wanted.append(jax.ShapeDtypeStruct((positions, sampled), F32))
    taken = (sample_row, connectivity.T, table, device_row, node_basis)
    *sent, owners = pl.pallas_call(
        functools.partial(owner_kernel, devices, groups, capacity, ndof),
        out_shape=tuple(wanted),
        in_specs=[pl.BlockSpec(memory_space=pltpu.HBM)] * 5,
        out_specs=(vmem,) * len(wanted),
        scratch_shapes=[pltpu.VMEM(x.shape, x.dtype) for x in taken] + [pltpu.SemaphoreType.DMA((4 + ndof,))],
        compiler_params=room(60),
        name="owner_rows",
    )(*taken)
    slots = lax.all_to_all(sent[-1], "elem", split_axis=0, concat_axis=0, tiled=True)
    got = slots if joined else lax.all_gather(sent[0], "elem", axis=0, tiled=True)

    rows_per = ROWS_PER_TABLE
    members = rows_per // pitch
    tables = (
        jax.ShapeDtypeStruct((quarter // members, rows_per, LANES), I32),
        jax.ShapeDtypeStruct((slot_rows, LANES), I32),
        jax.ShapeDtypeStruct((slot_rows, LANES), I32),
    )
    quarter_places, slot_places, slot_lane = pl.pallas_call(
        functools.partial(table_kernel, ndof, pitch, groups),
        out_shape=tables,
        in_specs=[vmem] * 2,
        out_specs=(vmem,) * 3,
        compiler_params=room(8, *tables),
        name="place_tables",
    )(owners, device_row)
    mine = pl.pallas_call(
        functools.partial(element_kernel, ndof, pitch),
        out_shape=jax.ShapeDtypeStruct((snaps + 2 * pitch, quarter * pitch), BF16),
        in_specs=[vmem] * 3,
        out_specs=vmem,
        compiler_params=room(12, got, quarter_places),
        name="element_squares",
    )(got, coords, quarter_places)
    every = lax.all_gather(mine, "snap", axis=0)

    return pl.pallas_call(
        functools.partial(panel_kernel, ndof, pitch, total_rows),
        out_shape=(
            jax.ShapeDtypeStruct((capacity, band, columns), F32),
            jax.ShapeDtypeStruct((columns // devices, columns), F32),
        ),
        in_specs=[vmem] * 5,
        out_specs=(pl.BlockSpec(memory_space=pl.ANY), vmem),
        scratch_shapes=[
            pltpu.VMEM(((chunk_lanes + slot_rows) // LANES, columns, LANES), F32),
            pltpu.VMEM((3, columns, chunk_lanes), BF16),
            pltpu.VMEM((columns, columns), F32),
            pltpu.VMEM((columns, slot_rows), F32),
            pltpu.VMEM((columns, columns), F32),
            pltpu.VMEM((BLOCK, columns), F32),
            pltpu.VMEM((2, BLOCK // STEP, 2 + 2 * STEP, STEP, LANES), F32),
            pltpu.VMEM((capacity, band, columns), F32),
            pltpu.SemaphoreType.DMA((slot_rows // LANES,)),
        ],
        compiler_params=room(30, every, slot_places),
        name="panel",
    )(every, slots, slot_places, slot_lane, stiff_terms)


def solution(mesh):
    placed = (P("elem", None), P(), P(None, "snap"), P(), P(), P(), P())
    return jax.shard_map(
        shards,
        mesh=mesh,
        in_specs=placed,
        out_specs=(P("elem", "snap", None), P("elem", None)),
        check_vma=False,
    )
```

```python
import functools

import jax
import jax.numpy as jnp
from jax import lax
from jax.experimental import pallas as pl
from jax.experimental.pallas import tpu as pltpu
from jax.sharding import PartitionSpec as P

F32, BF16, I32 = jnp.float32, jnp.bfloat16, jnp.int32
NT = (((1,), (1,)), ((), ()))
NN = (((1,), (0,)), ((), ()))
TN = (((0,), (0,)), ((), ()))
LANES = 128
TILE = 256
BLOCK = 128
PANEL = 64
STEP = 8
MEBI = 1 << 20
JOINED_LIMIT = 1 << 22
ROWS_PER_TABLE = 512
CHUNK = 8


def dot(a, b, dims=NN):
    return lax.dot_general(a, b, dims, preferred_element_type=F32)


def split(x):
    high = x.astype(BF16)
    return high, (x - high.astype(F32)).astype(BF16)


def dot3(a, b, dims=NN):
    (ah, al), (bh, bl) = a, b
    return dot(ah, bh, dims) + (dot(ah, bl, dims) + dot(al, bh, dims))


def iota(shape, dim):
    return lax.broadcasted_iota(I32, shape, dim)


def quotient(x, n):
    return jnp.floor((x.astype(F32) + 0.5) * (1.0 / n)).astype(I32)


def node_places(sample, links, table):
    positions, elems = links.shape
    sampled = sample.shape[1]
    pick = (iota((elems, sampled), 0) == sample).astype(F32).astype(BF16)
    shifted = links + 1
    parts = jnp.concatenate([(shifted >> 8).astype(F32), (shifted & 255).astype(F32)], axis=0)
    found = dot(parts.astype(BF16), pick)
    nodes = (found[:positions] * 256.0 + found[positions:]).astype(I32) - 1
    halves = jnp.concatenate([(table >> 8).astype(F32), (table & 255).astype(F32)], axis=1).T.astype(BF16)
    high, low = jnp.maximum(nodes, 0) >> 7, jnp.maximum(nodes, 0) & (LANES - 1)
    places = jnp.zeros((positions, sampled), F32)
    for p in range(positions):
        rows = (iota((table.shape[0], sampled), 0) == high[p : p + 1]).astype(F32).astype(BF16)
        both = dot(halves, rows)
        here = iota((LANES, sampled), 0) == low[p : p + 1]
        value = both[:LANES] * 256.0 + both[LANES:]
        value = jnp.sum(jnp.where(here, value, 0.0), axis=0, keepdims=True)
        places = jnp.where(iota((positions, sampled), 0) == p, value, places)
    return jnp.where(nodes >= 0, places, -1.0)


def slot_picks(elem_device, device, capacity):
    sampled = elem_device.shape[1]
    mine = (elem_device == device).astype(F32)
    before = (iota((sampled, sampled), 0) < iota((sampled, sampled), 1)).astype(F32).astype(BF16)
    ranks = dot(jnp.broadcast_to(mine, (16, sampled)).astype(BF16), before)[0:1]
    return jnp.where(iota((capacity, sampled), 0).astype(F32) == ranks, mine, 0.0)


def owner_kernel(devices, groups, capacity, ndof, *refs):
    inputs, outputs = refs[:5], refs[5:-6]
    *held, basis, sems = refs[-6:]
    shared, slots, owners = outputs[0], outputs[-2], outputs[-1]
    sample, links, table, elem_device = held[:4]
    modes = basis.shape[1] // ndof
    copies = [pltpu.make_async_copy(ref, to, sems.at[n]) for n, (ref, to) in enumerate(zip(inputs[:4], held))]
    for c in range(ndof):
        part = slice(c * modes, (c + 1) * modes)
        copies.append(pltpu.make_async_copy(inputs[4].at[:, part], basis.at[:, part], sems.at[4 + c]))
    for copy in copies:
        copy.start()
    elem_rank, snap_rank = lax.axis_index("elem"), lax.axis_index("snap")
    node_rows = basis.shape[0]
    band = modes // groups
    sampled = sample.shape[1]
    quarter = sampled // groups
    first = slots.shape[1] - capacity
    for copy in copies[:4]:
        copy.wait()
    places = node_places(sample[...], links[...], table[...])
    owner = jnp.floor((places + 0.5) * (1.0 / node_rows))
    owners[...] = jnp.where(places >= 0, owner, -1.0)
    here = (places >= 0) & (owner == elem_rank.astype(F32))
    local = places - (elem_rank * node_rows).astype(F32) + 1.0
    local = jnp.sum(jnp.where(here, local, 0.0), axis=0, keepdims=True)
    wanted = (iota((quarter, sampled), 1) == iota((quarter, sampled), 0) + snap_rank * quarter).astype(F32)
    picks = [wanted] + [slot_picks(elem_device[...], d, capacity) for d in range(devices)]
    row = jnp.sum(jnp.concatenate(picks, axis=0) * local, axis=1, keepdims=True).astype(I32) - 1
    pick = (iota((row.shape[0], node_rows), 1) == row).astype(F32).astype(BF16)
    for c in range(ndof):
        copies[4 + c].wait()
        rows = dot(pick, basis[:, c * modes : (c + 1) * modes])
        full = rows[:quarter].astype(BF16)
        part = jnp.zeros((devices * capacity, band), F32)
        for k in range(groups):
            part = jnp.where(snap_rank == k, rows[quarter:, k * band : (k + 1) * band], part)
        part = part.astype(BF16)
        for d in range(shared.shape[0]):
            shared[d, c * quarter : (c + 1) * quarter, :] = full
        for d in range(devices):
            slots[d, first:, c * band : (c + 1) * band] = part[d * capacity : (d + 1) * capacity]
    for d in range(devices):
        slots[d, first:, ndof * band :] = jnp.zeros((capacity, modes - ndof * band), BF16)


def place_targets(owner_col, ndof, pitch, live, members):
    index = iota(owner_col.shape, 0)
    member, row = index // pitch, index % pitch
    position = quotient(row, ndof)
    dof = row - position * ndof
    target = (owner_col.astype(I32) * ndof + dof) * members + member
    target = jnp.where((owner_col >= 0) & (row < live), target, -1)
    return jnp.broadcast_to(target, (owner_col.shape[0], LANES))


def one_hot(targets, lane_count, start=0):
    rows = targets.shape[0]
    wide = [iota((rows, LANES), 1) + (start + at) == targets for at in range(0, lane_count, LANES)]
    return jnp.concatenate([w.astype(F32).astype(BF16) for w in wide], axis=1)


def owner_rows(owners, rows, ndof, pitch):
    positions = owners.shape[0]
    position = quotient(iota((rows, positions), 0) % pitch, ndof)
    pick = (position == iota((rows, positions), 1)).astype(F32).astype(BF16)
    return dot(pick, owners.astype(BF16))


def table_kernel(
    ndof, pitch, groups, owners, elem_device, stiff, quarter_places, slot_places, slot_lane, terms_wide
):
    elem_rank, snap_rank = lax.axis_index("elem"), lax.axis_index("snap")
    positions, sampled = owners.shape
    live = positions * ndof
    quarter = sampled // groups
    parts, rows, _ = quarter_places.shape
    members = rows // pitch
    own = owner_rows(owners[...], rows, ndof, pitch)
    for h in range(parts):
        first = snap_rank * quarter + h * members
        at = iota((rows, sampled), 1) == iota((rows, sampled), 0) // pitch + first
        owner_col = jnp.sum(jnp.where(at, own, 0.0), axis=1, keepdims=True)
        quarter_places[h] = place_targets(owner_col, ndof, pitch, live, members)

    rows = slot_places.shape[0]
    capacity = rows // pitch
    picks = slot_picks(elem_device[...], elem_rank, capacity)
    member = iota((rows, capacity), 0) // pitch
    expand = (member == iota((rows, capacity), 1)).astype(F32).astype(BF16)
    picks = dot(expand, picks.astype(BF16))
    own = owner_rows(owners[...], rows, ndof, pitch)
    owner_col = jnp.sum(picks * (own + 1.0), axis=1, keepdims=True) - 1.0
    slot_places[...] = place_targets(owner_col, ndof, pitch, live, capacity)
    which = jnp.sum(picks * (iota((rows, sampled), 1) + 1).astype(F32), axis=1, keepdims=True).astype(I32) - 1
    lane = which * pitch + iota((rows, 1), 0) % pitch
    slot_lane[...] = jnp.broadcast_to(jnp.where(which >= 0, lane, -1), (rows, LANES))

    tile_of = (iota((live, TILE), 1) % pitch == iota((live, TILE), 0)).astype(F32).astype(BF16)
    diagonal = iota((TILE, TILE), 0) // pitch == iota((TILE, TILE), 1) // pitch
    for t in range(stiff.shape[0]):
        wide = dot(stiff[t], tile_of)
        wide = jnp.concatenate([wide, jnp.zeros((pitch - live, TILE), F32)], axis=0)
        wide = jnp.concatenate([wide] * (TILE // pitch), axis=0)
        terms_wide[t] = jnp.where(diagonal, wide, 0.0).astype(BF16)


def element_kernel(ndof, pitch, got, coords, places, out):
    devices = got.shape[0]
    parts, rows, _ = places.shape
    members = rows // pitch
    quarter = parts * members
    snaps = out.shape[0] - 2 * pitch
    per_tile = TILE // pitch
    for h in range(parts):
        source = jnp.concatenate(
            [
                got[o, c * quarter + h * members : c * quarter + (h + 1) * members, :]
                for o in range(devices)
                for c in range(ndof)
            ],
            axis=0,
        )
        basis = dot(one_hot(places[h], source.shape[0]), source).astype(BF16)
        moved = dot(coords[...], basis, NT).astype(BF16)
        out[0:snaps, h * rows : (h + 1) * rows] = moved
        for g in range(rows // TILE):
            part = basis[g * TILE : (g + 1) * TILE]
            square = dot(part, part, NT)
            block = jnp.zeros((pitch, TILE), F32)
            for i in range(per_tile):
                inside = iota((pitch, TILE), 1) // pitch == i
                block = jnp.where(inside, square[i * pitch : (i + 1) * pitch], block)
            high, low = split(block)
            lanes = slice(h * rows + g * TILE, h * rows + (g + 1) * TILE)
            out[snaps : snaps + pitch, lanes] = high
            out[snaps + pitch :, lanes] = low


def spread(x):
    return jnp.broadcast_to(x, (STEP, LANES))


def factor_block(block, rows, work):
    count, per = BLOCK // STEP, PANEL // STEP
    span = range(STEP)
    left = [block[STEP * c : STEP * c + STEP] for c in range(count)]
    right = [
        (iota((STEP, LANES), 1) == iota((STEP, LANES), 0) + STEP * c).astype(F32) for c in range(count)
    ]
    sub = iota((STEP, LANES), 0)

    def columns_of(c, base):
        return [spread(left[c][:, base + k : base + k + 1]) for k in span]

    upper, inverse = [], []
    work = list(work)
    own = None
    for j in range(count):
        base = STEP * j
        end = (j // per + 1) * per
        rows[j, 0], rows[j, 1] = left[j], right[j]
        ul = [spread(rows[j, 0, k : k + 1]) for k in span]
        ur = [spread(rows[j, 1, k : k + 1]) for k in span]
        own = columns_of(j, base) if own is None else own
        for k in span:
            rows[j, 2 + k] = own[k]
        s = {(i, k): spread(rows[j, 2 + k, i : i + 1]) for k in span for i in range(k, STEP)}
        below = {c: columns_of(c, base) for c in range(j + 1, end)}
        next_own = columns_of(j + 1, base + STEP) if j + 1 < end else None
        low = {}
        out_l, out_r = jnp.zeros((STEP, LANES), F32), jnp.zeros((STEP, LANES), F32)
        for k in span:
            root = lax.rsqrt(s[k, k])
            for i in range(k + 1, STEP):
                low[i, k] = s[i, k] * root
            for m in range(k + 1, STEP):
                for i in range(m, STEP):
                    s[i, m] = s[i, m] - low[i, k] * low[m, k]
            ul[k], ur[k] = ul[k] * root, ur[k] * root
            for i in range(k + 1, STEP):
                ul[i] = ul[i] - low[i, k] * ul[k]
                ur[i] = ur[i] - low[i, k] * ur[k]
            out_l = jnp.where(sub == k, ul[k], out_l)
            out_r = jnp.where(sub == k, ur[k], out_r)
            scaled = {}
            for c, col in below.items():
                scaled[c] = col[k] * root
                for i in range(k + 1, STEP):
                    col[i] = col[i] - scaled[c] * low[i, k]
                left[c] = left[c] - scaled[c] * ul[k]
                right[c] = right[c] - scaled[c] * ur[k]
            if next_own is not None:
                rows[j, 2 + STEP + k] = scaled[j + 1]
                for i in span:
                    other = spread(rows[j, 2 + STEP + k, i : i + 1])
                    next_own[i] = next_own[i] - scaled[j + 1] * other
        own = next_own
        keep = iota((STEP, LANES), 1) >= sub + base
        upper.append(jnp.where(keep, out_l, 0.0))
        inverse.append(out_r)
        if j + 1 == end and end < count:
            lh, ll = split(jnp.concatenate(upper[end - per : end], axis=0))
            rh, rl = split(jnp.concatenate(inverse[end - per : end], axis=0))
            both_h, both_l = jnp.concatenate([lh, rh], axis=1), jnp.concatenate([ll, rl], axis=1)
            update = dot(
                jnp.concatenate([lh, lh, ll], axis=0), jnp.concatenate([both_h, both_l, both_h], axis=0), TN
            )
            for c in range(end, count):
                left[c] = left[c] - update[STEP * c : STEP * c + STEP, :LANES]
                right[c] = right[c] - update[STEP * c : STEP * c + STEP, LANES:]
        for _ in range(-(-len(work) // (count - j))):
            work.pop(0)()
    return jnp.concatenate(upper, axis=0), jnp.concatenate(inverse, axis=0)


def cut(b):
    return slice(b * BLOCK, (b + 1) * BLOCK)


def factorize(gram, side, lower, rows, work):
    count = gram.shape[0] // BLOCK
    block = gram[cut(0), cut(0)]
    for b in range(count):
        top, inverse = factor_block(block, rows.at[b % 2], work)
        lower[cut(b), cut(b)] = top.T
        inverse, down, across, work = split(inverse), {}, {}, []

        def below(r, b=b, inverse=inverse, down=down):
            value = dot3(split(gram[cut(r), cut(b)]), inverse, NT)
            lower[cut(r), cut(b)] = value
            down[r] = split(value)

        def update(r, c, down=down):
            gram[cut(r), cut(c)] = gram[cut(r), cut(c)] - dot3(down[r], down[c], NT)

        def solve(h, b=b, inverse=inverse, across=across):
            value = dot3(inverse, split(side[cut(b), h : h + TILE]))
            side[cut(b), h : h + TILE] = value
            across[h] = split(value)

        def reduce(r, h, down=down, across=across):
            side[cut(r), h : h + TILE] = side[cut(r), h : h + TILE] - dot3(down[r], across[h])

        if b + 1 < count:
            below(b + 1)
            block = gram[cut(b + 1), cut(b + 1)] - dot3(down[b + 1], down[b + 1], NT)
        work = [functools.partial(below, r) for r in range(b + 2, count)]
        work += [functools.partial(update, r, c) for r in range(b + 2, count) for c in range(b + 1, r + 1)]
        for h in range(0, side.shape[1], TILE):
            work.append(functools.partial(solve, h))
            work += [functools.partial(reduce, r, h) for r in range(b + 1, count)]
    for step in work:
        step()


def panel_kernel(
    ndof, pitch, total_rows, every, got, places, slot_lane, terms_wide, panel, factor, forces, halves, squares, gram,
    side, lower, turned, rows, result, sems,
):
    elem_rank = lax.axis_index("elem")
    groups, height, lanes = every.shape
    snaps = height - 2 * pitch
    terms = terms_wide.shape[0]
    columns = snaps * terms
    blocks = columns // BLOCK
    capacity, band, _ = panel.shape
    devices = got.shape[0]
    per_tile, per_group = TILE // pitch, lanes // TILE
    tiles = [(q, t) for q in range(groups) for t in range(per_group)]
    slot_rows = capacity * pitch
    diagonal = iota((TILE, TILE), 0) // pitch == iota((TILE, TILE), 1) // pitch
    held = {}

    def piece_of(q, t, first, count):
        return every[q, first : first + count, pl.ds(pl.multiple_of(t * TILE, TILE), TILE)]

    def put_forces(moved, first):
        count = moved.shape[0] // snaps
        for t in range(terms):
            force = dot(moved, terms_wide[t], NT)
            for n in range(count):
                for h in range(TILE // LANES):
                    piece = force[n * snaps : (n + 1) * snaps, h * LANES : (h + 1) * LANES]
                    forces[(first + n) * TILE // LANES + h, pl.ds(t, snaps, stride=terms), :] = piece

    def start_chunk(part):
        put_forces(jnp.concatenate([piece_of(q, t, 0, snaps) for q, t in part], axis=0), 0)
        for n, (q, t) in enumerate(part):
            for low in (0, 1):
                square = piece_of(q, t, snaps + low * pitch, pitch).astype(F32)
                wide = jnp.concatenate([square] * per_tile, axis=0)
                squares[low, n] = jnp.where(diagonal, wide, 0.0).astype(BF16)

    def multiply(b, n):
        force = [forces[n * TILE // LANES + h, cut(b)] for h in range(TILE // LANES)]
        force = jnp.concatenate(force, axis=1).astype(BF16)
        here = slice(n * TILE, (n + 1) * TILE)
        halves[0, cut(b), here] = force
        halves[1, cut(b), here], halves[2, cut(b), here] = split(
            dot(force, squares[0, n]) + dot(force, squares[1, n])
        )

    def add_gram(b, count, fresh):
        end, upto = count * TILE, (b + 1) * BLOCK
        term = dot(halves[0, cut(b), :end], halves[1, :upto, :end], NT)
        term = term + dot(halves[0, cut(b), :end], halves[2, :upto, :end], NT)
        term = term * (1.0 / total_rows)
        gram[cut(b), :upto] = term if fresh else gram[cut(b), :upto] + term

    def chunk_work(b, count, fresh):
        work = [functools.partial(multiply, b, n) for n in range(count)]
        return work + [functools.partial(add_gram, b, count, fresh)]

    def slot_displaced():
        moved = jnp.zeros((snaps, slot_rows), F32)
        for n, (q, t) in enumerate(tiles):
            moved = moved + dot(piece_of(q, t, 0, snaps), one_hot(slot_lane[...], TILE, n * TILE), NT)
        moved = moved.astype(BF16)
        moved = [moved[:, t * TILE : (t + 1) * TILE] for t in range(slot_rows // TILE)]
        held["moved"] = jnp.concatenate(moved, axis=0)

    def slot_forces():
        put_forces(held["moved"], CHUNK)
        for h in range(slot_rows // LANES):
            side[:, h * LANES : (h + 1) * LANES] = forces[CHUNK * TILE // LANES + h].astype(BF16).astype(F32)

    def slot_basis():
        first = got.shape[1] - capacity
        source = jnp.concatenate(
            [got[o, first:, c * band : (c + 1) * band] for o in range(devices) for c in range(ndof)], axis=0
        )
        held["basis"] = dot(one_hot(places[...], source.shape[0]), source).T

    def clear():
        for b in range(blocks):
            for c in range(b):
                lower[cut(c), cut(b)] = jnp.zeros((BLOCK, BLOCK), F32)

    slot_work = [slot_displaced, slot_forces, slot_basis, clear]
    if len(tiles) <= CHUNK:
        start_chunk(tiles)
        for step in chunk_work(0, len(tiles), True):
            step()
        work = [step for b in range(1, blocks) for step in chunk_work(b, len(tiles), True)] + slot_work
    else:
        gram[...] = jnp.zeros_like(gram)

        @pl.loop(0, len(tiles) // CHUNK)
        def _(step):
            numbers = [step * CHUNK + n for n in range(CHUNK)]
            start_chunk([(n // per_group, n % per_group) for n in numbers])
            for b in range(blocks):
                for work in chunk_work(b, CHUNK, False):
                    work()

        work = slot_work
    factorize(gram, side, lower, rows, work)

    share = factor.shape[0]
    block = elem_rank * share // BLOCK
    columns_here = lower[:, pl.ds(pl.multiple_of(block * BLOCK, BLOCK), BLOCK)]
    turned[...] = columns_here.T
    factor[...] = turned[pl.ds(pl.multiple_of(elem_rank * share - block * BLOCK, share), share), :]

    each = LANES // pitch
    copies = []
    for n in range(slot_rows // LANES):
        high, low = split(side[:, n * LANES : (n + 1) * LANES])
        right = jnp.concatenate([high, low], axis=1)
        piece = held["basis"][:, n * LANES : (n + 1) * LANES]
        left = jnp.concatenate(
            [jnp.where(iota((band, LANES), 1) // pitch == i, piece, 0.0) for i in range(each)], axis=0
        ).astype(BF16)
        values = dot(jnp.concatenate([left, left], axis=1), right, NT)
        for i in range(each):
            result[n * each + i] = values[i * band : (i + 1) * band]
        here = pl.ds(n * each, each)
        copies.append(pltpu.make_async_copy(result.at[here], panel.at[here], sems.at[n]))
        copies[-1].start()
    for copy in copies:
        copy.wait()


def room(mebi, *arrays):
    size = sum(2 * a.size * a.dtype.itemsize for a in arrays)
    return pltpu.CompilerParams(vmem_limit_bytes=min(60 * MEBI, mebi * MEBI + size))


def shards(node_basis, stiff_terms, reduced_coords, sample_list, connectivity, node_slot, elem_device):
    devices = lax.axis_size("elem")
    groups = lax.axis_size("snap")
    node_rows, width = node_basis.shape
    modes, local_snaps = reduced_coords.shape
    snaps = local_snaps * groups
    ndof = width // modes
    terms, live, _ = stiff_terms.shape
    sampled = sample_list.shape[0]
    positions = connectivity.shape[1]
    capacity = 2 * sampled // devices
    quarter = sampled // groups
    pitch = 32
    band = modes // groups
    columns = snaps * terms
    total_rows = sampled * modes
    chunk_lanes = CHUNK * TILE
    slot_rows = capacity * pitch

    vmem = pl.BlockSpec(memory_space=pltpu.VMEM)

    coords = lax.all_gather(reduced_coords.T, "snap", axis=0, tiled=True)
    sample_row = sample_list.reshape(1, sampled)
    device_row = elem_device.reshape(1, sampled)
    table = node_slot.reshape(-1, LANES)
    shared_rows = ndof * quarter
    joined = devices * (shared_rows + capacity) * modes <= JOINED_LIMIT
    if joined:
        sent = ((devices, shared_rows + capacity, modes),)
    else:
        sent = ((1, shared_rows, modes), (devices, capacity, modes))
    wanted = [jax.ShapeDtypeStruct(shape, BF16) for shape in sent]
    wanted.append(jax.ShapeDtypeStruct((positions, sampled), F32))
    taken = (sample_row, connectivity.T, table, device_row, node_basis)
    *sent, owners = pl.pallas_call(
        functools.partial(owner_kernel, devices, groups, capacity, ndof),
        out_shape=tuple(wanted),
        in_specs=[pl.BlockSpec(memory_space=pltpu.HBM)] * 5,
        out_specs=(vmem,) * len(wanted),
        scratch_shapes=[pltpu.VMEM(x.shape, x.dtype) for x in taken] + [pltpu.SemaphoreType.DMA((4 + ndof,))],
        compiler_params=room(60),
        name="owner_rows",
    )(*taken)
    slots = lax.all_to_all(sent[-1], "elem", split_axis=0, concat_axis=0, tiled=True)
    got = slots if joined else lax.all_gather(sent[0], "elem", axis=0, tiled=True)

    rows_per = ROWS_PER_TABLE
    members = rows_per // pitch
    tables = (
        jax.ShapeDtypeStruct((quarter // members, rows_per, LANES), I32),
        jax.ShapeDtypeStruct((slot_rows, LANES), I32),
        jax.ShapeDtypeStruct((slot_rows, LANES), I32),
        jax.ShapeDtypeStruct((terms, TILE, TILE), BF16),
    )
    quarter_places, slot_places, slot_lane, terms_wide = pl.pallas_call(
        functools.partial(table_kernel, ndof, pitch, groups),
        out_shape=tables,
        in_specs=[vmem] * 3,
        out_specs=(vmem,) * 4,
        compiler_params=room(14, *tables),
        name="place_tables",
    )(owners, device_row, stiff_terms)
    mine = pl.pallas_call(
        functools.partial(element_kernel, ndof, pitch),
        out_shape=jax.ShapeDtypeStruct((snaps + 2 * pitch, quarter * pitch), BF16),
        in_specs=[vmem] * 3,
        out_specs=vmem,
        compiler_params=room(12, got, quarter_places),
        name="element_squares",
    )(got, coords, quarter_places)
    every = lax.all_gather(mine, "snap", axis=0)

    return pl.pallas_call(
        functools.partial(panel_kernel, ndof, pitch, total_rows),
        out_shape=(
            jax.ShapeDtypeStruct((capacity, band, columns), F32),
            jax.ShapeDtypeStruct((columns // devices, columns), F32),
        ),
        in_specs=[vmem] * 5,
        out_specs=(pl.BlockSpec(memory_space=pl.ANY), vmem),
        scratch_shapes=[
            pltpu.VMEM(((chunk_lanes + slot_rows) // LANES, columns, LANES), F32),
            pltpu.VMEM((3, columns, chunk_lanes), BF16),
            pltpu.VMEM((2, CHUNK, TILE, TILE), BF16),
            pltpu.VMEM((columns, columns), F32),
            pltpu.VMEM((columns, slot_rows), F32),
            pltpu.VMEM((columns, columns), F32),
            pltpu.VMEM((BLOCK, columns), F32),
            pltpu.VMEM((2, BLOCK // STEP, 2 + 2 * STEP, STEP, LANES), F32),
            pltpu.VMEM((capacity, band, columns), F32),
            pltpu.SemaphoreType.DMA((slot_rows // LANES,)),
        ],
        compiler_params=room(34, every, slot_places),
        name="panel",
    )(every, slots, slot_places, slot_lane, terms_wide)


def solution(mesh):
    placed = (P("elem", None), P(), P(None, "snap"), P(), P(), P(), P())
    return jax.shard_map(
        shards,
        mesh=mesh,
        in_specs=placed,
        out_specs=(P("elem", "snap", None), P("elem", None)),
        check_vma=False,
    )
```

```python
import functools

import jax
import jax.numpy as jnp
from jax import lax
from jax.experimental import pallas as pl
from jax.experimental.pallas import tpu as pltpu
from jax.sharding import PartitionSpec as P

F32, BF16, I32 = jnp.float32, jnp.bfloat16, jnp.int32
NT = (((1,), (1,)), ((), ()))
NN = (((1,), (0,)), ((), ()))
TN = (((0,), (0,)), ((), ()))
LANES = 128
TILE = 256
BLOCK = 128
PANEL = 64
STEP = 8
MEBI = 1 << 20
JOINED_LIMIT = 1 << 22
ROWS_PER_TABLE = 512
CHUNK = 8


def dot(a, b, dims=NN):
    return lax.dot_general(a, b, dims, preferred_element_type=F32)


def split(x):
    high = x.astype(BF16)
    return high, (x - high.astype(F32)).astype(BF16)


def dot3(a, b, dims=NN):
    (ah, al), (bh, bl) = a, b
    (along,), (across,) = dims[0]
    left = jnp.concatenate([ah, ah, al], axis=along)
    return dot(left, jnp.concatenate([bh, bl, bh], axis=across), dims)


def iota(shape, dim):
    return lax.broadcasted_iota(I32, shape, dim)


def quotient(x, n):
    return jnp.floor((x.astype(F32) + 0.5) * (1.0 / n)).astype(I32)


def node_places(sample, links, table):
    positions, elems = links.shape
    sampled = sample.shape[1]
    pick = (iota((elems, sampled), 0) == sample).astype(F32).astype(BF16)
    shifted = links + 1
    parts = jnp.concatenate([(shifted >> 8).astype(F32), (shifted & 255).astype(F32)], axis=0)
    found = dot(parts.astype(BF16), pick)
    nodes = (found[:positions] * 256.0 + found[positions:]).astype(I32) - 1
    halves = jnp.concatenate([(table >> 8).astype(F32), (table & 255).astype(F32)], axis=1).T.astype(BF16)
    high, low = jnp.maximum(nodes, 0) >> 7, jnp.maximum(nodes, 0) & (LANES - 1)
    places = jnp.zeros((positions, sampled), F32)
    for p in range(positions):
        rows = (iota((table.shape[0], sampled), 0) == high[p : p + 1]).astype(F32).astype(BF16)
        both = dot(halves, rows)
        here = iota((LANES, sampled), 0) == low[p : p + 1]
        value = both[:LANES] * 256.0 + both[LANES:]
        value = jnp.sum(jnp.where(here, value, 0.0), axis=0, keepdims=True)
        places = jnp.where(iota((positions, sampled), 0) == p, value, places)
    return jnp.where(nodes >= 0, places, -1.0)


def slot_picks(elem_device, device, capacity):
    sampled = elem_device.shape[1]
    mine = (elem_device == device).astype(F32)
    before = (iota((sampled, sampled), 0) < iota((sampled, sampled), 1)).astype(F32).astype(BF16)
    ranks = dot(jnp.broadcast_to(mine, (16, sampled)).astype(BF16), before)[0:1]
    return jnp.where(iota((capacity, sampled), 0).astype(F32) == ranks, mine, 0.0)


def owner_kernel(devices, groups, capacity, ndof, *refs):
    inputs, outputs = refs[:5], refs[5:-6]
    *held, basis, sems = refs[-6:]
    shared, slots, owners = outputs[0], outputs[-2], outputs[-1]
    sample, links, table, elem_device = held[:4]
    modes = basis.shape[1] // ndof
    copies = [pltpu.make_async_copy(ref, to, sems.at[n]) for n, (ref, to) in enumerate(zip(inputs[:4], held))]
    for c in range(ndof):
        part = slice(c * modes, (c + 1) * modes)
        copies.append(pltpu.make_async_copy(inputs[4].at[:, part], basis.at[:, part], sems.at[4 + c]))
    for copy in copies:
        copy.start()
    elem_rank, snap_rank = lax.axis_index("elem"), lax.axis_index("snap")
    node_rows = basis.shape[0]
    band = modes // groups
    sampled = sample.shape[1]
    quarter = sampled // groups
    first = slots.shape[1] - capacity
    for copy in copies[:4]:
        copy.wait()
    places = node_places(sample[...], links[...], table[...])
    owner = jnp.floor((places + 0.5) * (1.0 / node_rows))
    owners[...] = jnp.where(places >= 0, owner, -1.0)
    here = (places >= 0) & (owner == elem_rank.astype(F32))
    local = places - (elem_rank * node_rows).astype(F32) + 1.0
    local = jnp.sum(jnp.where(here, local, 0.0), axis=0, keepdims=True)
    wanted = (iota((quarter, sampled), 1) == iota((quarter, sampled), 0) + snap_rank * quarter).astype(F32)
    picks = [wanted] + [slot_picks(elem_device[...], d, capacity) for d in range(devices)]
    row = jnp.sum(jnp.concatenate(picks, axis=0) * local, axis=1, keepdims=True).astype(I32) - 1
    pick = (iota((row.shape[0], node_rows), 1) == row).astype(F32).astype(BF16)
    for c in range(ndof):
        copies[4 + c].wait()
        rows = dot(pick, basis[:, c * modes : (c + 1) * modes])
        full = rows[:quarter].astype(BF16)
        part = jnp.zeros((devices * capacity, band), F32)
        for k in range(groups):
            part = jnp.where(snap_rank == k, rows[quarter:, k * band : (k + 1) * band], part)
        part = part.astype(BF16)
        for d in range(shared.shape[0]):
            shared[d, c * quarter : (c + 1) * quarter, :] = full
        for d in range(devices):
            slots[d, first:, c * band : (c + 1) * band] = part[d * capacity : (d + 1) * capacity]
    for d in range(devices):
        slots[d, first:, ndof * band :] = jnp.zeros((capacity, modes - ndof * band), BF16)


def place_targets(owner_col, ndof, pitch, live, members):
    index = iota(owner_col.shape, 0)
    member, row = index // pitch, index % pitch
    position = quotient(row, ndof)
    dof = row - position * ndof
    target = (owner_col.astype(I32) * ndof + dof) * members + member
    target = jnp.where((owner_col >= 0) & (row < live), target, -1)
    return jnp.broadcast_to(target, (owner_col.shape[0], LANES))


def one_hot(targets, lane_count, start=0):
    rows = targets.shape[0]
    wide = [iota((rows, LANES), 1) + (start + at) == targets for at in range(0, lane_count, LANES)]
    return jnp.concatenate([w.astype(F32).astype(BF16) for w in wide], axis=1)


def owner_rows(owners, rows, ndof, pitch):
    positions = owners.shape[0]
    position = quotient(iota((rows, positions), 0) % pitch, ndof)
    pick = (position == iota((rows, positions), 1)).astype(F32).astype(BF16)
    return dot(pick, owners.astype(BF16))


def table_kernel(
    ndof, pitch, groups, owners, elem_device, stiff, quarter_places, slot_places, slot_lane, terms_wide
):
    elem_rank, snap_rank = lax.axis_index("elem"), lax.axis_index("snap")
    positions, sampled = owners.shape
    live = positions * ndof
    quarter = sampled // groups
    parts, rows, _ = quarter_places.shape
    members = rows // pitch
    own = owner_rows(owners[...], rows, ndof, pitch)
    for h in range(parts):
        first = snap_rank * quarter + h * members
        at = iota((rows, sampled), 1) == iota((rows, sampled), 0) // pitch + first
        owner_col = jnp.sum(jnp.where(at, own, 0.0), axis=1, keepdims=True)
        quarter_places[h] = place_targets(owner_col, ndof, pitch, live, members)

    rows = slot_places.shape[0]
    capacity = rows // pitch
    picks = slot_picks(elem_device[...], elem_rank, capacity)
    member = iota((rows, capacity), 0) // pitch
    expand = (member == iota((rows, capacity), 1)).astype(F32).astype(BF16)
    picks = dot(expand, picks.astype(BF16))
    own = owner_rows(owners[...], rows, ndof, pitch)
    owner_col = jnp.sum(picks * (own + 1.0), axis=1, keepdims=True) - 1.0
    slot_places[...] = place_targets(owner_col, ndof, pitch, live, capacity)
    which = jnp.sum(picks * (iota((rows, sampled), 1) + 1).astype(F32), axis=1, keepdims=True).astype(I32) - 1
    lane = which * pitch + iota((rows, 1), 0) % pitch
    slot_lane[...] = jnp.broadcast_to(jnp.where(which >= 0, lane, -1), (rows, LANES))

    tile_of = (iota((live, TILE), 1) % pitch == iota((live, TILE), 0)).astype(F32).astype(BF16)
    diagonal = iota((TILE, TILE), 0) // pitch == iota((TILE, TILE), 1) // pitch
    for t in range(stiff.shape[0]):
        wide = dot(stiff[t], tile_of)
        wide = jnp.concatenate([wide, jnp.zeros((pitch - live, TILE), F32)], axis=0)
        wide = jnp.concatenate([wide] * (TILE // pitch), axis=0)
        terms_wide[t] = jnp.where(diagonal, wide, 0.0).astype(BF16)


def element_kernel(ndof, pitch, got, coords, places, out):
    devices = got.shape[0]
    parts, rows, _ = places.shape
    members = rows // pitch
    quarter = parts * members
    snaps = out.shape[0] - 2 * pitch
    per_tile = TILE // pitch
    for h in range(parts):
        source = jnp.concatenate(
            [
                got[o, c * quarter + h * members : c * quarter + (h + 1) * members, :]
                for o in range(devices)
                for c in range(ndof)
            ],
            axis=0,
        )
        basis = dot(one_hot(places[h], source.shape[0]), source).astype(BF16)
        moved = dot(coords[...], basis, NT).astype(BF16)
        out[0:snaps, h * rows : (h + 1) * rows] = moved
        for g in range(rows // TILE):
            part = basis[g * TILE : (g + 1) * TILE]
            square = dot(part, part, NT)
            block = jnp.zeros((pitch, TILE), F32)
            for i in range(per_tile):
                inside = iota((pitch, TILE), 1) // pitch == i
                block = jnp.where(inside, square[i * pitch : (i + 1) * pitch], block)
            high, low = split(block)
            lanes = slice(h * rows + g * TILE, h * rows + (g + 1) * TILE)
            out[snaps : snaps + pitch, lanes] = high
            out[snaps + pitch :, lanes] = low


def spread(x):
    return jnp.broadcast_to(x, (STEP, LANES))


def factor_block(block, rows, work):
    count, per = BLOCK // STEP, PANEL // STEP
    span = range(STEP)
    left = [block[STEP * c : STEP * c + STEP] for c in range(count)]
    right = [
        (iota((STEP, LANES), 1) == iota((STEP, LANES), 0) + STEP * c).astype(F32) for c in range(count)
    ]
    sub = iota((STEP, LANES), 0)

    def columns_of(c, base):
        return [spread(left[c][:, base + k : base + k + 1]) for k in span]

    upper, inverse = [], []
    work = list(work)
    own = None
    for j in range(count):
        base = STEP * j
        end = (j // per + 1) * per
        rows[j, 0], rows[j, 1] = left[j], right[j]
        ul = [spread(rows[j, 0, k : k + 1]) for k in span]
        ur = [spread(rows[j, 1, k : k + 1]) for k in span]
        own = columns_of(j, base) if own is None else own
        for k in span:
            rows[j, 2 + k] = own[k]
        s = {(i, k): spread(rows[j, 2 + k, i : i + 1]) for k in span for i in range(k, STEP)}
        below = {c: columns_of(c, base) for c in range(j + 1, end)}
        next_own = columns_of(j + 1, base + STEP) if j + 1 < end else None
        low = {}
        out_l, out_r = jnp.zeros((STEP, LANES), F32), jnp.zeros((STEP, LANES), F32)
        for k in span:
            root = lax.rsqrt(s[k, k])
            for i in range(k + 1, STEP):
                low[i, k] = s[i, k] * root
            for m in range(k + 1, STEP):
                for i in range(m, STEP):
                    s[i, m] = s[i, m] - low[i, k] * low[m, k]
            ul[k], ur[k] = ul[k] * root, ur[k] * root
            for i in range(k + 1, STEP):
                ul[i] = ul[i] - low[i, k] * ul[k]
                ur[i] = ur[i] - low[i, k] * ur[k]
            out_l = jnp.where(sub == k, ul[k], out_l)
            out_r = jnp.where(sub == k, ur[k], out_r)
            scaled = {}
            for c, col in below.items():
                scaled[c] = col[k] * root
                for i in range(k + 1, STEP):
                    col[i] = col[i] - scaled[c] * low[i, k]
                left[c] = left[c] - scaled[c] * ul[k]
                right[c] = right[c] - scaled[c] * ur[k]
            if next_own is not None:
                rows[j, 2 + STEP + k] = scaled[j + 1]
                for i in span:
                    other = spread(rows[j, 2 + STEP + k, i : i + 1])
                    next_own[i] = next_own[i] - scaled[j + 1] * other
        own = next_own
        keep = iota((STEP, LANES), 1) >= sub + base
        upper.append(jnp.where(keep, out_l, 0.0))
        inverse.append(out_r)
        if j + 1 == end and end < count:
            lh, ll = split(jnp.concatenate(upper[end - per : end], axis=0))
            rh, rl = split(jnp.concatenate(inverse[end - per : end], axis=0))
            both_h, both_l = jnp.concatenate([lh, rh], axis=1), jnp.concatenate([ll, rl], axis=1)
            update = dot(
                jnp.concatenate([lh, lh, ll], axis=0), jnp.concatenate([both_h, both_l, both_h], axis=0), TN
            )
            for c in range(end, count):
                left[c] = left[c] - update[STEP * c : STEP * c + STEP, :LANES]
                right[c] = right[c] - update[STEP * c : STEP * c + STEP, LANES:]
        for _ in range(-(-len(work) // (count - j))):
            work.pop(0)()
    return jnp.concatenate(upper, axis=0), jnp.concatenate(inverse, axis=0)


def cut(b):
    return slice(b * BLOCK, (b + 1) * BLOCK)


def factorize(gram, side, lower, rows, work):
    count = gram.shape[0] // BLOCK
    block = gram[cut(0), cut(0)]
    for b in range(count):
        top, inverse = factor_block(block, rows.at[b % 2], work)
        lower[cut(b), cut(b)] = top.T
        inverse, down, across, work = split(inverse), {}, {}, []

        def below(r, b=b, inverse=inverse, down=down):
            value = dot3(split(gram[cut(r), cut(b)]), inverse, NT)
            lower[cut(r), cut(b)] = value
            down[r] = split(value)

        def update(r, c, down=down):
            gram[cut(r), cut(c)] = gram[cut(r), cut(c)] - dot3(down[r], down[c], NT)

        def solve(h, b=b, inverse=inverse, across=across):
            value = dot3(inverse, split(side[cut(b), h : h + TILE]))
            side[cut(b), h : h + TILE] = value
            across[h] = split(value)

        def reduce(r, h, down=down, across=across):
            side[cut(r), h : h + TILE] = side[cut(r), h : h + TILE] - dot3(down[r], across[h])

        if b + 1 < count:
            below(b + 1)
            block = gram[cut(b + 1), cut(b + 1)] - dot3(down[b + 1], down[b + 1], NT)
        work = [functools.partial(below, r) for r in range(b + 2, count)]
        work += [functools.partial(update, r, c) for r in range(b + 2, count) for c in range(b + 1, r + 1)]
        for h in range(0, side.shape[1], TILE):
            work.append(functools.partial(solve, h))
            work += [functools.partial(reduce, r, h) for r in range(b + 1, count)]
    for step in work:
        step()


def panel_kernel(
    ndof, pitch, total_rows, every, got, places, slot_lane, terms_wide, panel, factor, forces, halves, squares, gram,
    side, lower, turned, rows, result, sems,
):
    elem_rank = lax.axis_index("elem")
    groups, height, lanes = every.shape
    snaps = height - 2 * pitch
    terms = terms_wide.shape[0]
    columns = snaps * terms
    blocks = columns // BLOCK
    capacity, band, _ = panel.shape
    devices = got.shape[0]
    per_tile, per_group = TILE // pitch, lanes // TILE
    tiles = [(q, t) for q in range(groups) for t in range(per_group)]
    slot_rows = capacity * pitch
    diagonal = iota((TILE, TILE), 0) // pitch == iota((TILE, TILE), 1) // pitch
    held = {}

    def piece_of(q, t, first, count):
        return every[q, first : first + count, pl.ds(pl.multiple_of(t * TILE, TILE), TILE)]

    def put_forces(moved, first):
        count = moved.shape[0] // snaps
        for t in range(terms):
            force = dot(moved, terms_wide[t], NT)
            for n in range(count):
                for h in range(TILE // LANES):
                    piece = force[n * snaps : (n + 1) * snaps, h * LANES : (h + 1) * LANES]
                    forces[(first + n) * TILE // LANES + h, pl.ds(t, snaps, stride=terms), :] = piece

    def start_chunk(part):
        put_forces(jnp.concatenate([piece_of(q, t, 0, snaps) for q, t in part], axis=0), 0)
        for n, (q, t) in enumerate(part):
            for low in (0, 1):
                square = piece_of(q, t, snaps + low * pitch, pitch).astype(F32)
                wide = jnp.concatenate([square] * per_tile, axis=0)
                squares[low, n] = jnp.where(diagonal, wide, 0.0).astype(BF16)

    def multiply(b, n):
        force = [forces[n * TILE // LANES + h, cut(b)] for h in range(TILE // LANES)]
        force = jnp.concatenate(force, axis=1).astype(BF16)
        here = slice(n * TILE, (n + 1) * TILE)
        halves[0, cut(b), here] = force
        both = jnp.concatenate([squares[0, n], squares[1, n]], axis=0)
        halves[1, cut(b), here], halves[2, cut(b), here] = split(dot(jnp.concatenate([force, force], axis=1), both))

    def add_gram(b, count, fresh):
        end, upto = count * TILE, (b + 1) * BLOCK
        force = halves[0, cut(b), :end]
        both = jnp.concatenate([halves[1, :upto, :end], halves[2, :upto, :end]], axis=1)
        term = dot(jnp.concatenate([force, force], axis=1), both, NT) * (1.0 / total_rows)
        gram[cut(b), :upto] = term if fresh else gram[cut(b), :upto] + term

    def chunk_work(b, count, fresh):
        work = [functools.partial(multiply, b, n) for n in range(count)]
        return work + [functools.partial(add_gram, b, count, fresh)]

    def slot_displaced():
        moved = jnp.zeros((snaps, slot_rows), F32)
        for n, (q, t) in enumerate(tiles):
            moved = moved + dot(piece_of(q, t, 0, snaps), one_hot(slot_lane[...], TILE, n * TILE), NT)
        moved = moved.astype(BF16)
        moved = [moved[:, t * TILE : (t + 1) * TILE] for t in range(slot_rows // TILE)]
        held["moved"] = jnp.concatenate(moved, axis=0)

    def slot_forces():
        put_forces(held["moved"], CHUNK)
        for h in range(slot_rows // LANES):
            force = forces[CHUNK * TILE // LANES + h, :columns]
            side[:, h * LANES : (h + 1) * LANES] = force.astype(BF16).astype(F32)

    def slot_basis():
        first = got.shape[1] - capacity
        source = jnp.concatenate(
            [got[o, first:, c * band : (c + 1) * band] for o in range(devices) for c in range(ndof)], axis=0
        )
        held["basis"] = dot(one_hot(places[...], source.shape[0]), source).T

    def clear():
        for b in range(blocks):
            for c in range(b):
                lower[cut(c), cut(b)] = jnp.zeros((BLOCK, BLOCK), F32)

    slot_work = [slot_displaced, slot_forces, slot_basis, clear]
    if len(tiles) <= CHUNK:
        start_chunk(tiles)
        for step in chunk_work(0, len(tiles), True):
            step()
        work = [step for b in range(1, blocks) for step in chunk_work(b, len(tiles), True)] + slot_work
    else:
        gram[...] = jnp.zeros_like(gram)

        @pl.loop(0, len(tiles) // CHUNK)
        def _(step):
            numbers = [step * CHUNK + n for n in range(CHUNK)]
            start_chunk([(n // per_group, n % per_group) for n in numbers])
            for b in range(blocks):
                for work in chunk_work(b, CHUNK, False):
                    work()

        work = slot_work
    factorize(gram, side, lower, rows, work)

    share = factor.shape[0]
    block = elem_rank * share // BLOCK
    columns_here = lower[:, pl.ds(pl.multiple_of(block * BLOCK, BLOCK), BLOCK)]
    turned[...] = columns_here.T
    factor[...] = turned[pl.ds(pl.multiple_of(elem_rank * share - block * BLOCK, share), share), :]

    each = LANES // pitch
    copies = []
    for n in range(slot_rows // LANES):
        high, low = split(side[:, n * LANES : (n + 1) * LANES])
        right = jnp.concatenate([high, low], axis=1)
        piece = held["basis"][:, n * LANES : (n + 1) * LANES]
        left = jnp.concatenate(
            [jnp.where(iota((band, LANES), 1) // pitch == i, piece, 0.0) for i in range(each)], axis=0
        ).astype(BF16)
        values = dot(jnp.concatenate([left, left], axis=1), right, NT)
        for i in range(each):
            result[n * each + i] = values[i * band : (i + 1) * band]
        here = pl.ds(n * each, each)
        copies.append(pltpu.make_async_copy(result.at[here], panel.at[here], sems.at[n]))
        copies[-1].start()
    for copy in copies:
        copy.wait()


def room(mebi, *arrays):
    size = sum(2 * a.size * a.dtype.itemsize for a in arrays)
    return pltpu.CompilerParams(vmem_limit_bytes=min(60 * MEBI, mebi * MEBI + size))


def shards(node_basis, stiff_terms, reduced_coords, sample_list, connectivity, node_slot, elem_device):
    devices = lax.axis_size("elem")
    groups = lax.axis_size("snap")
    node_rows, width = node_basis.shape
    modes, local_snaps = reduced_coords.shape
    snaps = local_snaps * groups
    ndof = width // modes
    terms, live, _ = stiff_terms.shape
    sampled = sample_list.shape[0]
    positions = connectivity.shape[1]
    capacity = 2 * sampled // devices
    quarter = sampled // groups
    pitch = 32
    band = modes // groups
    columns = snaps * terms
    total_rows = sampled * modes
    chunk_lanes = CHUNK * TILE
    slot_rows = capacity * pitch

    vmem = pl.BlockSpec(memory_space=pltpu.VMEM)

    coords = lax.all_gather(reduced_coords.T, "snap", axis=0, tiled=True)
    sample_row = sample_list.reshape(1, sampled)
    device_row = elem_device.reshape(1, sampled)
    table = node_slot.reshape(-1, LANES)
    shared_rows = ndof * quarter
    joined = devices * (shared_rows + capacity) * modes <= JOINED_LIMIT
    if joined:
        sent = ((devices, shared_rows + capacity, modes),)
    else:
        sent = ((1, shared_rows, modes), (devices, capacity, modes))
    wanted = [jax.ShapeDtypeStruct(shape, BF16) for shape in sent]
    wanted.append(jax.ShapeDtypeStruct((positions, sampled), F32))
    taken = (sample_row, connectivity.T, table, device_row, node_basis)
    *sent, owners = pl.pallas_call(
        functools.partial(owner_kernel, devices, groups, capacity, ndof),
        out_shape=tuple(wanted),
        in_specs=[pl.BlockSpec(memory_space=pltpu.HBM)] * 5,
        out_specs=(vmem,) * len(wanted),
        scratch_shapes=[pltpu.VMEM(x.shape, x.dtype) for x in taken] + [pltpu.SemaphoreType.DMA((4 + ndof,))],
        compiler_params=room(60),
        name="owner_rows",
    )(*taken)
    slots = lax.all_to_all(sent[-1], "elem", split_axis=0, concat_axis=0, tiled=True)
    got = slots if joined else lax.all_gather(sent[0], "elem", axis=0, tiled=True)

    rows_per = ROWS_PER_TABLE
    members = rows_per // pitch
    tables = (
        jax.ShapeDtypeStruct((quarter // members, rows_per, LANES), I32),
        jax.ShapeDtypeStruct((slot_rows, LANES), I32),
        jax.ShapeDtypeStruct((slot_rows, LANES), I32),
        jax.ShapeDtypeStruct((terms, TILE, TILE), BF16),
    )
    quarter_places, slot_places, slot_lane, terms_wide = pl.pallas_call(
        functools.partial(table_kernel, ndof, pitch, groups),
        out_shape=tables,
        in_specs=[vmem] * 3,
        out_specs=(vmem,) * 4,
        compiler_params=room(14, *tables),
        name="place_tables",
    )(owners, device_row, stiff_terms)
    mine = pl.pallas_call(
        functools.partial(element_kernel, ndof, pitch),
        out_shape=jax.ShapeDtypeStruct((snaps + 2 * pitch, quarter * pitch), BF16),
        in_specs=[vmem] * 3,
        out_specs=vmem,
        compiler_params=room(12, got, quarter_places),
        name="element_squares",
    )(got, coords, quarter_places)
    every = lax.all_gather(mine, "snap", axis=0)

    return pl.pallas_call(
        functools.partial(panel_kernel, ndof, pitch, total_rows),
        out_shape=(
            jax.ShapeDtypeStruct((capacity, band, columns), F32),
            jax.ShapeDtypeStruct((columns // devices, columns), F32),
        ),
        in_specs=[vmem] * 5,
        out_specs=(pl.BlockSpec(memory_space=pl.ANY), vmem),
        scratch_shapes=[
            pltpu.VMEM(((chunk_lanes + slot_rows) // LANES, columns + terms, LANES), F32),
            pltpu.VMEM((3, columns, chunk_lanes), BF16),
            pltpu.VMEM((2, CHUNK, TILE, TILE), BF16),
            pltpu.VMEM((columns, columns), F32),
            pltpu.VMEM((columns, slot_rows), F32),
            pltpu.VMEM((columns, columns), F32),
            pltpu.VMEM((BLOCK, columns), F32),
            pltpu.VMEM((2, BLOCK // STEP, 2 + 2 * STEP, STEP, LANES), F32),
            pltpu.VMEM((capacity, band, columns), F32),
            pltpu.SemaphoreType.DMA((slot_rows // LANES,)),
        ],
        compiler_params=room(34, every, slot_places),
        name="panel",
    )(every, slots, slot_places, slot_lane, terms_wide)


def solution(mesh):
    placed = (P("elem", None), P(), P(None, "snap"), P(), P(), P(), P())
    return jax.shard_map(
        shards,
        mesh=mesh,
        in_specs=placed,
        out_specs=(P("elem", "snap", None), P("elem", None)),
        check_vma=False,
    )
```

```python
import functools

import jax
import jax.numpy as jnp
from jax import lax
from jax.experimental import pallas as pl
from jax.experimental.pallas import tpu as pltpu
from jax.sharding import PartitionSpec as P

F32, BF16, I32 = jnp.float32, jnp.bfloat16, jnp.int32
NT = (((1,), (1,)), ((), ()))
NN = (((1,), (0,)), ((), ()))
TN = (((0,), (0,)), ((), ()))
LANES = 128
TILE = 256
BLOCK = 128
PANEL = 32
STEP = 8
MEBI = 1 << 20
JOINED_LIMIT = 1 << 22
ROWS_PER_TABLE = 512
CHUNK = 8


def dot(a, b, dims=NN):
    return lax.dot_general(a, b, dims, preferred_element_type=F32)


def split(x):
    high = x.astype(BF16)
    return high, (x - high.astype(F32)).astype(BF16)


def dot3(a, b, dims=NN):
    (ah, al), (bh, bl) = a, b
    (along,), (across,) = dims[0]
    left = jnp.concatenate([ah, ah, al], axis=along)
    return dot(left, jnp.concatenate([bh, bl, bh], axis=across), dims)


def iota(shape, dim):
    return lax.broadcasted_iota(I32, shape, dim)


def quotient(x, n):
    return jnp.floor((x.astype(F32) + 0.5) * (1.0 / n)).astype(I32)


def node_places(sample, links, table):
    positions, elems = links.shape
    sampled = sample.shape[1]
    pick = (iota((elems, sampled), 0) == sample).astype(F32).astype(BF16)
    shifted = links + 1
    parts = jnp.concatenate([(shifted >> 8).astype(F32), (shifted & 255).astype(F32)], axis=0)
    found = dot(parts.astype(BF16), pick)
    nodes = (found[:positions] * 256.0 + found[positions:]).astype(I32) - 1
    halves = jnp.concatenate([(table >> 8).astype(F32), (table & 255).astype(F32)], axis=1).T.astype(BF16)
    high, low = jnp.maximum(nodes, 0) >> 7, jnp.maximum(nodes, 0) & (LANES - 1)
    places = jnp.zeros((positions, sampled), F32)
    for p in range(positions):
        rows = (iota((table.shape[0], sampled), 0) == high[p : p + 1]).astype(F32).astype(BF16)
        both = dot(halves, rows)
        here = iota((LANES, sampled), 0) == low[p : p + 1]
        value = both[:LANES] * 256.0 + both[LANES:]
        value = jnp.sum(jnp.where(here, value, 0.0), axis=0, keepdims=True)
        places = jnp.where(iota((positions, sampled), 0) == p, value, places)
    return jnp.where(nodes >= 0, places, -1.0)


def slot_picks(elem_device, device, capacity):
    sampled = elem_device.shape[1]
    mine = (elem_device == device).astype(F32)
    before = (iota((sampled, sampled), 0) < iota((sampled, sampled), 1)).astype(F32).astype(BF16)
    ranks = dot(jnp.broadcast_to(mine, (16, sampled)).astype(BF16), before)[0:1]
    return jnp.where(iota((capacity, sampled), 0).astype(F32) == ranks, mine, 0.0)


def owner_kernel(devices, groups, capacity, ndof, *refs):
    inputs, outputs = refs[:5], refs[5:-6]
    *held, basis, sems = refs[-6:]
    shared, slots, owners = outputs[0], outputs[-2], outputs[-1]
    sample, links, table, elem_device = held[:4]
    modes = basis.shape[1] // ndof
    copies = [pltpu.make_async_copy(ref, to, sems.at[n]) for n, (ref, to) in enumerate(zip(inputs[:4], held))]
    for c in range(ndof):
        part = slice(c * modes, (c + 1) * modes)
        copies.append(pltpu.make_async_copy(inputs[4].at[:, part], basis.at[:, part], sems.at[4 + c]))
    for copy in copies:
        copy.start()
    elem_rank, snap_rank = lax.axis_index("elem"), lax.axis_index("snap")
    node_rows = basis.shape[0]
    band = modes // groups
    sampled = sample.shape[1]
    quarter = sampled // groups
    first = slots.shape[1] - capacity
    for copy in copies[:4]:
        copy.wait()
    places = node_places(sample[...], links[...], table[...])
    owner = jnp.floor((places + 0.5) * (1.0 / node_rows))
    owners[...] = jnp.where(places >= 0, owner, -1.0)
    here = (places >= 0) & (owner == elem_rank.astype(F32))
    local = places - (elem_rank * node_rows).astype(F32) + 1.0
    local = jnp.sum(jnp.where(here, local, 0.0), axis=0, keepdims=True)
    wanted = (iota((quarter, sampled), 1) == iota((quarter, sampled), 0) + snap_rank * quarter).astype(F32)
    picks = [wanted] + [slot_picks(elem_device[...], d, capacity) for d in range(devices)]
    row = jnp.sum(jnp.concatenate(picks, axis=0) * local, axis=1, keepdims=True).astype(I32) - 1
    pick = (iota((row.shape[0], node_rows), 1) == row).astype(F32).astype(BF16)
    for c in range(ndof):
        copies[4 + c].wait()
        rows = dot(pick, basis[:, c * modes : (c + 1) * modes])
        full = rows[:quarter].astype(BF16)
        part = jnp.zeros((devices * capacity, band), F32)
        for k in range(groups):
            part = jnp.where(snap_rank == k, rows[quarter:, k * band : (k + 1) * band], part)
        part = part.astype(BF16)
        for d in range(shared.shape[0]):
            shared[d, c * quarter : (c + 1) * quarter, :] = full
        for d in range(devices):
            slots[d, first:, c * band : (c + 1) * band] = part[d * capacity : (d + 1) * capacity]
    for d in range(devices):
        slots[d, first:, ndof * band :] = jnp.zeros((capacity, modes - ndof * band), BF16)


def place_targets(owner_col, ndof, pitch, live, members):
    index = iota(owner_col.shape, 0)
    member, row = index // pitch, index % pitch
    position = quotient(row, ndof)
    dof = row - position * ndof
    target = (owner_col.astype(I32) * ndof + dof) * members + member
    target = jnp.where((owner_col >= 0) & (row < live), target, -1)
    return jnp.broadcast_to(target, (owner_col.shape[0], LANES))


def one_hot(targets, lane_count, start=0):
    rows = targets.shape[0]
    wide = [iota((rows, LANES), 1) + (start + at) == targets for at in range(0, lane_count, LANES)]
    return jnp.concatenate([w.astype(F32).astype(BF16) for w in wide], axis=1)


def owner_rows(owners, rows, ndof, pitch):
    positions = owners.shape[0]
    position = quotient(iota((rows, positions), 0) % pitch, ndof)
    pick = (position == iota((rows, positions), 1)).astype(F32).astype(BF16)
    return dot(pick, owners.astype(BF16))


def table_kernel(
    ndof, pitch, groups, owners, elem_device, stiff, quarter_places, slot_places, slot_lane, terms_wide
):
    elem_rank, snap_rank = lax.axis_index("elem"), lax.axis_index("snap")
    positions, sampled = owners.shape
    live = positions * ndof
    quarter = sampled // groups
    parts, rows, _ = quarter_places.shape
    members = rows // pitch
    own = owner_rows(owners[...], rows, ndof, pitch)
    for h in range(parts):
        first = snap_rank * quarter + h * members
        at = iota((rows, sampled), 1) == iota((rows, sampled), 0) // pitch + first
        owner_col = jnp.sum(jnp.where(at, own, 0.0), axis=1, keepdims=True)
        quarter_places[h] = place_targets(owner_col, ndof, pitch, live, members)

    rows = slot_places.shape[0]
    capacity = rows // pitch
    picks = slot_picks(elem_device[...], elem_rank, capacity)
    member = iota((rows, capacity), 0) // pitch
    expand = (member == iota((rows, capacity), 1)).astype(F32).astype(BF16)
    picks = dot(expand, picks.astype(BF16))
    own = owner_rows(owners[...], rows, ndof, pitch)
    owner_col = jnp.sum(picks * (own + 1.0), axis=1, keepdims=True) - 1.0
    slot_places[...] = place_targets(owner_col, ndof, pitch, live, capacity)
    which = jnp.sum(picks * (iota((rows, sampled), 1) + 1).astype(F32), axis=1, keepdims=True).astype(I32) - 1
    lane = which * pitch + iota((rows, 1), 0) % pitch
    slot_lane[...] = jnp.broadcast_to(jnp.where(which >= 0, lane, -1), (rows, LANES))

    tile_of = (iota((live, TILE), 1) % pitch == iota((live, TILE), 0)).astype(F32).astype(BF16)
    diagonal = iota((TILE, TILE), 0) // pitch == iota((TILE, TILE), 1) // pitch
    for t in range(stiff.shape[0]):
        wide = dot(stiff[t], tile_of)
        wide = jnp.concatenate([wide, jnp.zeros((pitch - live, TILE), F32)], axis=0)
        wide = jnp.concatenate([wide] * (TILE // pitch), axis=0)
        terms_wide[t] = jnp.where(diagonal, wide, 0.0).astype(BF16)


def element_kernel(ndof, pitch, got, coords, places, out):
    devices = got.shape[0]
    parts, rows, _ = places.shape
    members = rows // pitch
    quarter = parts * members
    snaps = out.shape[0] - 2 * pitch
    per_tile = TILE // pitch
    for h in range(parts):
        source = jnp.concatenate(
            [
                got[o, c * quarter + h * members : c * quarter + (h + 1) * members, :]
                for o in range(devices)
                for c in range(ndof)
            ],
            axis=0,
        )
        basis = dot(one_hot(places[h], source.shape[0]), source).astype(BF16)
        moved = dot(coords[...], basis, NT).astype(BF16)
        out[0:snaps, h * rows : (h + 1) * rows] = moved
        for g in range(rows // TILE):
            part = basis[g * TILE : (g + 1) * TILE]
            square = dot(part, part, NT)
            block = jnp.zeros((pitch, TILE), F32)
            for i in range(per_tile):
                inside = iota((pitch, TILE), 1) // pitch == i
                block = jnp.where(inside, square[i * pitch : (i + 1) * pitch], block)
            high, low = split(block)
            lanes = slice(h * rows + g * TILE, h * rows + (g + 1) * TILE)
            out[snaps : snaps + pitch, lanes] = high
            out[snaps + pitch :, lanes] = low


def spread(x):
    return jnp.broadcast_to(x, (STEP, LANES))


def factor_block(block, rows, work):
    count, per = BLOCK // STEP, PANEL // STEP
    span = range(STEP)
    left = [block[STEP * c : STEP * c + STEP] for c in range(count)]
    right = [
        (iota((STEP, LANES), 1) == iota((STEP, LANES), 0) + STEP * c).astype(F32) for c in range(count)
    ]
    sub = iota((STEP, LANES), 0)

    def columns_of(c, base):
        return [spread(left[c][:, base + k : base + k + 1]) for k in span]

    upper, inverse = [], []
    work = list(work)
    own = None
    for j in range(count):
        base = STEP * j
        end = (j // per + 1) * per
        rows[j, 0], rows[j, 1] = left[j], right[j]
        ul = [spread(rows[j, 0, k : k + 1]) for k in span]
        ur = [spread(rows[j, 1, k : k + 1]) for k in span]
        own = columns_of(j, base) if own is None else own
        for k in span:
            rows[j, 2 + k] = own[k]
        s = {(i, k): spread(rows[j, 2 + k, i : i + 1]) for k in span for i in range(k, STEP)}
        below = {c: columns_of(c, base) for c in range(j + 1, end)}
        next_own = columns_of(j + 1, base + STEP) if j + 1 < end else None
        low = {}
        out_l, out_r = jnp.zeros((STEP, LANES), F32), jnp.zeros((STEP, LANES), F32)
        for k in span:
            root = lax.rsqrt(s[k, k])
            for i in range(k + 1, STEP):
                low[i, k] = s[i, k] * root
            for m in range(k + 1, STEP):
                for i in range(m, STEP):
                    s[i, m] = s[i, m] - low[i, k] * low[m, k]
            ul[k], ur[k] = ul[k] * root, ur[k] * root
            for i in range(k + 1, STEP):
                ul[i] = ul[i] - low[i, k] * ul[k]
                ur[i] = ur[i] - low[i, k] * ur[k]
            out_l = jnp.where(sub == k, ul[k], out_l)
            out_r = jnp.where(sub == k, ur[k], out_r)
            scaled = {}
            for c, col in below.items():
                scaled[c] = col[k] * root
                for i in range(k + 1, STEP):
                    col[i] = col[i] - scaled[c] * low[i, k]
                left[c] = left[c] - scaled[c] * ul[k]
                right[c] = right[c] - scaled[c] * ur[k]
            if next_own is not None:
                rows[j, 2 + STEP + k] = scaled[j + 1]
                for i in span:
                    other = spread(rows[j, 2 + STEP + k, i : i + 1])
                    next_own[i] = next_own[i] - scaled[j + 1] * other
        own = next_own
        keep = iota((STEP, LANES), 1) >= sub + base
        upper.append(jnp.where(keep, out_l, 0.0))
        inverse.append(out_r)
        if j + 1 == end and end < count:
            lh, ll = split(jnp.concatenate(upper[end - per : end], axis=0))
            rh, rl = split(jnp.concatenate(inverse[end - per : end], axis=0))
            both_h, both_l = jnp.concatenate([lh, rh], axis=1), jnp.concatenate([ll, rl], axis=1)
            update = dot(
                jnp.concatenate([lh, lh, ll], axis=0), jnp.concatenate([both_h, both_l, both_h], axis=0), TN
            )
            for c in range(end, count):
                left[c] = left[c] - update[STEP * c : STEP * c + STEP, :LANES]
                right[c] = right[c] - update[STEP * c : STEP * c + STEP, LANES:]
        for _ in range(-(-len(work) // (count - j))):
            work.pop(0)()
    return jnp.concatenate(upper, axis=0), jnp.concatenate(inverse, axis=0)


def cut(b):
    return slice(b * BLOCK, (b + 1) * BLOCK)


def factorize(gram, side, lower, rows, work):
    count = gram.shape[0] // BLOCK
    block = gram[cut(0), cut(0)]
    for b in range(count):
        top, inverse = factor_block(block, rows.at[b % 2], work)
        lower[cut(b), cut(b)] = top.T
        inverse, down, across, work = split(inverse), {}, {}, []

        def below(r, b=b, inverse=inverse, down=down):
            value = dot3(split(gram[cut(r), cut(b)]), inverse, NT)
            lower[cut(r), cut(b)] = value
            down[r] = split(value)

        def update(r, c, down=down):
            gram[cut(r), cut(c)] = gram[cut(r), cut(c)] - dot3(down[r], down[c], NT)

        def solve(h, b=b, inverse=inverse, across=across):
            value = dot3(inverse, split(side[cut(b), h : h + TILE]))
            side[cut(b), h : h + TILE] = value
            across[h] = split(value)

        def reduce(r, h, down=down, across=across):
            side[cut(r), h : h + TILE] = side[cut(r), h : h + TILE] - dot3(down[r], across[h])

        if b + 1 < count:
            below(b + 1)
            block = gram[cut(b + 1), cut(b + 1)] - dot3(down[b + 1], down[b + 1], NT)
        work = [functools.partial(below, r) for r in range(b + 2, count)]
        work += [functools.partial(update, r, c) for r in range(b + 2, count) for c in range(b + 1, r + 1)]
        for h in range(0, side.shape[1], TILE):
            work.append(functools.partial(solve, h))
            work += [functools.partial(reduce, r, h) for r in range(b + 1, count)]
    for step in work:
        step()


def panel_kernel(
    ndof, pitch, total_rows, every, got, places, slot_lane, terms_wide, panel, factor, forces, halves, squares, gram,
    side, lower, turned, rows, result, sems,
):
    elem_rank = lax.axis_index("elem")
    groups, height, lanes = every.shape
    snaps = height - 2 * pitch
    terms = terms_wide.shape[0]
    columns = snaps * terms
    blocks = columns // BLOCK
    capacity, band, _ = panel.shape
    devices = got.shape[0]
    per_tile, per_group = TILE // pitch, lanes // TILE
    tiles = [(q, t) for q in range(groups) for t in range(per_group)]
    slot_rows = capacity * pitch
    diagonal = iota((TILE, TILE), 0) // pitch == iota((TILE, TILE), 1) // pitch
    held = {}

    def piece_of(q, t, first, count):
        return every[q, first : first + count, pl.ds(pl.multiple_of(t * TILE, TILE), TILE)]

    def put_forces(moved, first):
        count = moved.shape[0] // snaps
        for t in range(terms):
            force = dot(moved, terms_wide[t], NT)
            for n in range(count):
                for h in range(TILE // LANES):
                    piece = force[n * snaps : (n + 1) * snaps, h * LANES : (h + 1) * LANES]
                    forces[(first + n) * TILE // LANES + h, pl.ds(t, snaps, stride=terms), :] = piece

    def start_chunk(part):
        put_forces(jnp.concatenate([piece_of(q, t, 0, snaps) for q, t in part], axis=0), 0)
        for n, (q, t) in enumerate(part):
            for low in (0, 1):
                square = piece_of(q, t, snaps + low * pitch, pitch).astype(F32)
                wide = jnp.concatenate([square] * per_tile, axis=0)
                squares[low, n] = jnp.where(diagonal, wide, 0.0).astype(BF16)

    def multiply(b, n):
        force = [forces[n * TILE // LANES + h, cut(b)] for h in range(TILE // LANES)]
        force = jnp.concatenate(force, axis=1).astype(BF16)
        here = slice(n * TILE, (n + 1) * TILE)
        halves[0, cut(b), here] = force
        both = jnp.concatenate([squares[0, n], squares[1, n]], axis=0)
        halves[1, cut(b), here], halves[2, cut(b), here] = split(dot(jnp.concatenate([force, force], axis=1), both))

    def add_gram(b, count, fresh):
        end, upto = count * TILE, (b + 1) * BLOCK
        force = halves[0, cut(b), :end]
        both = jnp.concatenate([halves[1, :upto, :end], halves[2, :upto, :end]], axis=1)
        term = dot(jnp.concatenate([force, force], axis=1), both, NT) * (1.0 / total_rows)
        gram[cut(b), :upto] = term if fresh else gram[cut(b), :upto] + term

    def chunk_work(b, count, fresh):
        work = [functools.partial(multiply, b, n) for n in range(count)]
        return work + [functools.partial(add_gram, b, count, fresh)]

    def slot_displaced():
        moved = jnp.zeros((snaps, slot_rows), F32)
        for n, (q, t) in enumerate(tiles):
            moved = moved + dot(piece_of(q, t, 0, snaps), one_hot(slot_lane[...], TILE, n * TILE), NT)
        moved = moved.astype(BF16)
        moved = [moved[:, t * TILE : (t + 1) * TILE] for t in range(slot_rows // TILE)]
        held["moved"] = jnp.concatenate(moved, axis=0)

    def slot_forces():
        put_forces(held["moved"], CHUNK)
        for h in range(slot_rows // LANES):
            force = forces[CHUNK * TILE // LANES + h, :columns]
            side[:, h * LANES : (h + 1) * LANES] = force.astype(BF16).astype(F32)

    def slot_basis():
        first = got.shape[1] - capacity
        source = jnp.concatenate(
            [got[o, first:, c * band : (c + 1) * band] for o in range(devices) for c in range(ndof)], axis=0
        )
        held["basis"] = dot(one_hot(places[...], source.shape[0]), source).T

    def clear():
        for b in range(blocks):
            for c in range(b):
                lower[cut(c), cut(b)] = jnp.zeros((BLOCK, BLOCK), F32)

    slot_work = [slot_displaced, slot_forces, slot_basis, clear]
    if len(tiles) <= CHUNK:
        start_chunk(tiles)
        for step in chunk_work(0, len(tiles), True):
            step()
        work = [step for b in range(1, blocks) for step in chunk_work(b, len(tiles), True)] + slot_work
    else:
        gram[...] = jnp.zeros_like(gram)

        @pl.loop(0, len(tiles) // CHUNK)
        def _(step):
            numbers = [step * CHUNK + n for n in range(CHUNK)]
            start_chunk([(n // per_group, n % per_group) for n in numbers])
            for b in range(blocks):
                for work in chunk_work(b, CHUNK, False):
                    work()

        work = slot_work
    factorize(gram, side, lower, rows, work)

    share = factor.shape[0]
    block = elem_rank * share // BLOCK
    columns_here = lower[:, pl.ds(pl.multiple_of(block * BLOCK, BLOCK), BLOCK)]
    turned[...] = columns_here.T
    factor[...] = turned[pl.ds(pl.multiple_of(elem_rank * share - block * BLOCK, share), share), :]

    each = LANES // pitch
    copies = []
    for n in range(slot_rows // LANES):
        high, low = split(side[:, n * LANES : (n + 1) * LANES])
        right = jnp.concatenate([high, low], axis=1)
        piece = held["basis"][:, n * LANES : (n + 1) * LANES]
        left = jnp.concatenate(
            [jnp.where(iota((band, LANES), 1) // pitch == i, piece, 0.0) for i in range(each)], axis=0
        ).astype(BF16)
        values = dot(jnp.concatenate([left, left], axis=1), right, NT)
        for i in range(each):
            result[n * each + i] = values[i * band : (i + 1) * band]
        here = pl.ds(n * each, each)
        copies.append(pltpu.make_async_copy(result.at[here], panel.at[here], sems.at[n]))
        copies[-1].start()
    for copy in copies:
        copy.wait()


def room(mebi, *arrays):
    size = sum(2 * a.size * a.dtype.itemsize for a in arrays)
    return pltpu.CompilerParams(vmem_limit_bytes=min(60 * MEBI, mebi * MEBI + size))


def shards(node_basis, stiff_terms, reduced_coords, sample_list, connectivity, node_slot, elem_device):
    devices = lax.axis_size("elem")
    groups = lax.axis_size("snap")
    node_rows, width = node_basis.shape
    modes, local_snaps = reduced_coords.shape
    snaps = local_snaps * groups
    ndof = width // modes
    terms, live, _ = stiff_terms.shape
    sampled = sample_list.shape[0]
    positions = connectivity.shape[1]
    capacity = 2 * sampled // devices
    quarter = sampled // groups
    pitch = 32
    band = modes // groups
    columns = snaps * terms
    total_rows = sampled * modes
    chunk_lanes = CHUNK * TILE
    slot_rows = capacity * pitch

    vmem = pl.BlockSpec(memory_space=pltpu.VMEM)

    coords = lax.all_gather(reduced_coords.T, "snap", axis=0, tiled=True)
    sample_row = sample_list.reshape(1, sampled)
    device_row = elem_device.reshape(1, sampled)
    table = node_slot.reshape(-1, LANES)
    shared_rows = ndof * quarter
    joined = devices * (shared_rows + capacity) * modes <= JOINED_LIMIT
    if joined:
        sent = ((devices, shared_rows + capacity, modes),)
    else:
        sent = ((1, shared_rows, modes), (devices, capacity, modes))
    wanted = [jax.ShapeDtypeStruct(shape, BF16) for shape in sent]
    wanted.append(jax.ShapeDtypeStruct((positions, sampled), F32))
    taken = (sample_row, connectivity.T, table, device_row, node_basis)
    *sent, owners = pl.pallas_call(
        functools.partial(owner_kernel, devices, groups, capacity, ndof),
        out_shape=tuple(wanted),
        in_specs=[pl.BlockSpec(memory_space=pltpu.HBM)] * 5,
        out_specs=(vmem,) * len(wanted),
        scratch_shapes=[pltpu.VMEM(x.shape, x.dtype) for x in taken] + [pltpu.SemaphoreType.DMA((4 + ndof,))],
        compiler_params=room(60),
        name="owner_rows",
    )(*taken)
    slots = lax.all_to_all(sent[-1], "elem", split_axis=0, concat_axis=0, tiled=True)
    got = slots if joined else lax.all_gather(sent[0], "elem", axis=0, tiled=True)

    rows_per = ROWS_PER_TABLE
    members = rows_per // pitch
    tables = (
        jax.ShapeDtypeStruct((quarter // members, rows_per, LANES), I32),
        jax.ShapeDtypeStruct((slot_rows, LANES), I32),
        jax.ShapeDtypeStruct((slot_rows, LANES), I32),
        jax.ShapeDtypeStruct((terms, TILE, TILE), BF16),
    )
    quarter_places, slot_places, slot_lane, terms_wide = pl.pallas_call(
        functools.partial(table_kernel, ndof, pitch, groups),
        out_shape=tables,
        in_specs=[vmem] * 3,
        out_specs=(vmem,) * 4,
        compiler_params=room(14, *tables),
        name="place_tables",
    )(owners, device_row, stiff_terms)
    mine = pl.pallas_call(
        functools.partial(element_kernel, ndof, pitch),
        out_shape=jax.ShapeDtypeStruct((snaps + 2 * pitch, quarter * pitch), BF16),
        in_specs=[vmem] * 3,
        out_specs=vmem,
        compiler_params=room(12, got, quarter_places),
        name="element_squares",
    )(got, coords, quarter_places)
    every = lax.all_gather(mine, "snap", axis=0)

    return pl.pallas_call(
        functools.partial(panel_kernel, ndof, pitch, total_rows),
        out_shape=(
            jax.ShapeDtypeStruct((capacity, band, columns), F32),
            jax.ShapeDtypeStruct((columns // devices, columns), F32),
        ),
        in_specs=[vmem] * 5,
        out_specs=(pl.BlockSpec(memory_space=pl.ANY), vmem),
        scratch_shapes=[
            pltpu.VMEM(((chunk_lanes + slot_rows) // LANES, columns + terms, LANES), F32),
            pltpu.VMEM((3, columns, chunk_lanes), BF16),
            pltpu.VMEM((2, CHUNK, TILE, TILE), BF16),
            pltpu.VMEM((columns, columns), F32),
            pltpu.VMEM((columns, slot_rows), F32),
            pltpu.VMEM((columns, columns), F32),
            pltpu.VMEM((BLOCK, columns), F32),
            pltpu.VMEM((2, BLOCK // STEP, 2 + 2 * STEP, STEP, LANES), F32),
            pltpu.VMEM((capacity, band, columns), F32),
            pltpu.SemaphoreType.DMA((slot_rows // LANES,)),
        ],
        compiler_params=room(34, every, slot_places),
        name="panel",
    )(every, slots, slot_places, slot_lane, terms_wide)


def solution(mesh):
    placed = (P("elem", None), P(), P(None, "snap"), P(), P(), P(), P())
    return jax.shard_map(
        shards,
        mesh=mesh,
        in_specs=placed,
        out_specs=(P("elem", "snap", None), P("elem", None)),
        check_vma=False,
    )
```
